32 devices in a mesh: sec: 2 (over x), seq: 4 (over z), mp: 4 (over y, core).
Axes of the slice: x: 2, y: 2, z: 4, core: 2. Of those that a mesh axis runs over, the one named last changes fastest.
Arguments:
- queries: bfloat16 [1024, 2048], P(('sec', 'seq'), 'mp'), may hold values from -6 to 6
- keys_values: bfloat16 [2, 16, 2048], P(None, ('sec', 'seq'), 'mp'), may hold values from -6 to 6
- out_grad: bfloat16 [1024, 4096], P(('sec', 'seq'), 'mp'), may hold values from -6 to 6
- out_weight: bfloat16 [2048, 4096], P('mp'), may hold values from -0.125 to 0.125
- enc_len: int32 [2], replicated, may hold values from 4 to 8
- dec_len: int32 [2], replicated, may hold values from 1 to 512
Outputs:
- query_grad: bfloat16 [1024, 2048], P(('sec', 'seq'), 'mp')
- key_value_grad: bfloat16 [2, 16, 2048], P(None, ('sec', 'seq'), 'mp')
The draws below stay inside these ranges and needn't reach their ends.
All inputs are finite; a program needn't handle non-finite values.
Results may differ from the reference program's by a relative error of at most 0.014.
Values may be sent and summed in bfloat16 or wider, within the bound.
A program may use at most 64 MiB of HBM per device.

```python
import jax
import jax.numpy as jnp
from jax import lax

D = 4096
H = 8
DH = 256
SEQS = 2
TQ = 1024
SE = 16


def draw_queries(key, part):
    base = jnp.clip(jax.random.normal(jax.random.fold_in(key, 1), (TQ, H * DH), jnp.float32), -6.0, 6.0)
    return base.astype(jnp.bfloat16)


def draw_keys_values(key, part):
    base = jnp.clip(jax.random.normal(jax.random.fold_in(key, 2), (2, SE, H * DH), jnp.float32), -6.0, 6.0)
    return base.astype(jnp.bfloat16)


def levels(rng, dims, pieces, low, largest):
    def one(axis_at, shards_of):
        steps = jax.random.uniform(jax.random.fold_in(jax.random.fold_in(rng, 6), axis_at), (shards_of,), jnp.float32, low / len(pieces), largest / len(pieces))
        return jnp.repeat(jnp.exp(steps), dims[axis_at] // shards_of).reshape((-1,) + (1,) * (len(dims) - axis_at - 1))

    level = one(*pieces[0])
    for cut in pieces[1:]:
        level = level * one(*cut)
    return level


def scatter_about(rng, shape, scale, most, shards=(), held_as=jnp.bfloat16):
    loudness = levels(rng, shape, shards, -0.22, 0.18) if shards else 1.0
    array = jax.random.normal(rng, shape, jnp.float32) * scale * loudness
    return jnp.minimum(jnp.maximum(array, -most), most).astype(held_as)


def setup_inputs(seed: int = 0) -> dict:
    streams_of = jax.random.split(jax.random.key(seed), 7)
    return {
        "queries": draw_queries(jax.random.fold_in(streams_of[6], 71), 0),
        "keys_values": draw_keys_values(jax.random.fold_in(streams_of[6], 71), 0),
        "out_grad": scatter_about(streams_of[2], (TQ, D), 1.0, 6.0, ((0, 8), (1, 4))),
        "out_weight": scatter_about(streams_of[3], (H * DH, D), (H * DH) ** -0.5, 0.125, ((0, 4),)),
        "enc_len": jax.random.randint(streams_of[4], (SEQS,), max(2, SE // SEQS // 2), SE // SEQS + 1).astype(jnp.int32),
        "dec_len": jax.random.randint(streams_of[5], (SEQS,), 1, TQ // SEQS + 1).astype(jnp.int32),
    }


def reference(queries, keys_values, out_grad, out_weight, enc_len, dec_len):
    score_scale = DH ** -0.5
    total_q = queries.shape[0]
    total_k = keys_values.shape[1]
    per_query_seq = total_q // SEQS
    per_key_seq = total_k // SEQS
    query_pos = jnp.arange(total_q, dtype=jnp.int32)
    key_pos = jnp.arange(total_k, dtype=jnp.int32)
    query_seg = query_pos // per_query_seq
    key_seg = key_pos // per_key_seq
    key_valid = (key_pos % per_key_seq) < enc_len[key_seg]
    query_valid = (query_pos % per_query_seq) < dec_len[query_seg]
    allowed = (query_seg[:, None] == key_seg[None, :]) & key_valid[None, :]
    grad_heads = jnp.dot(out_grad, out_weight.T, preferred_element_type=jnp.float32).astype(jnp.bfloat16)
    grad_heads = jnp.where(query_valid[:, None], grad_heads, jnp.zeros_like(grad_heads))

    def one_head(head_index):
        first_col = head_index * DH
        q_head = lax.dynamic_slice_in_dim(queries, first_col, DH, 1)
        k_head = lax.dynamic_slice_in_dim(keys_values[0], first_col, DH, 1)
        v_head = lax.dynamic_slice_in_dim(keys_values[1], first_col, DH, 1)
        g_head = lax.dynamic_slice_in_dim(grad_heads, first_col, DH, 1)
        scores = jnp.dot(q_head, k_head.T, preferred_element_type=jnp.float32) * score_scale
        scores = jnp.where(allowed, scores, -1e30)
        row_max = jnp.max(scores, axis=1, keepdims=True)
        expo_terms = jnp.where(allowed, jnp.exp(scores - row_max), 0.0)
        log_total = row_max + jnp.log(jnp.sum(expo_terms, axis=1, keepdims=True))
        attn_prob = jnp.where(allowed, jnp.exp(scores - log_total), 0.0)
        attn_out = jnp.dot(attn_prob, v_head.astype(jnp.float32), precision=lax.Precision.HIGHEST)
        row_delta = jnp.sum(g_head.astype(jnp.float32) * attn_out, axis=1, keepdims=True)
        grad_prob = jnp.dot(g_head, v_head.T, preferred_element_type=jnp.float32)
        grad_score = (attn_prob * (grad_prob - row_delta)).astype(jnp.bfloat16)
        grad_query = (jnp.dot(grad_score, k_head, preferred_element_type=jnp.float32) * score_scale).astype(jnp.bfloat16)
        grad_key = (jnp.dot(grad_score.T, q_head, preferred_element_type=jnp.float32) * score_scale).astype(jnp.bfloat16)
        grad_value = jnp.dot(attn_prob.astype(jnp.bfloat16).T, g_head, preferred_element_type=jnp.float32).astype(jnp.bfloat16)
        return grad_query, grad_key, grad_value

    grad_query, grad_key, grad_value = lax.map(one_head, jnp.arange(H, dtype=jnp.int32))
    query_grad = jnp.transpose(grad_query, (1, 0, 2)).reshape(total_q, H * DH)
    key_grad = jnp.transpose(grad_key, (1, 0, 2)).reshape(total_k, H * DH)
    value_grad = jnp.transpose(grad_value, (1, 0, 2)).reshape(total_k, H * DH)
    return query_grad, jnp.stack([key_grad, value_grad])
```

```python
import functools

import jax
import jax.numpy as jnp
from jax import lax
from jax.experimental import pallas as pl
from jax.experimental.pallas import tpu as pltpu
from jax.sharding import PartitionSpec as P

DH = 256
SEQS = 2
MESH = pl.DeviceIdType.MESH
NN = (((1,), (0,)), ((), ()))
NT = (((1,), (1,)), ((), ()))
TN = (((0,), (0,)), ((), ()))


def dot(a, b, dims):
    return lax.dot_general(a, b, dims, preferred_element_type=jnp.float32)


def kernel(
    seq_n,
    mp_n,
    enc_ref,
    dec_ref,
    q_hbm,
    kv_hbm,
    x_hbm,
    w_hbm,
    qg_hbm,
    kvg_ref,
    q_buf,
    x_buf,
    w_buf,
    kv_all,
    k_rows,
    v_rows,
    p_all,
    vw_send,
    vw_all,
    gp_send,
    gp_all,
    t_send,
    t_all,
    kvg_send,
    kvg_all,
    qg_buf,
    q_sem,
    x_sem,
    w_sem,
    kv_own_sem,
    qg_sem,
    kv_s,
    kv_r,
    p_s,
    p_r,
    vw_s,
    vw_r,
    gp_s,
    gp_r,
    t_s,
    t_r,
    kvg_s,
    kvg_r,
):
    sec = lax.axis_index("sec")
    seq = lax.axis_index("seq")
    mp = lax.axis_index("mp")
    rows, width = q_buf.shape
    cols = x_buf.shape[1]
    own = kv_hbm.shape[1]
    heads = width // DH
    keys = own * seq_n
    kh = heads * keys

    chips = mp_n // 2
    chip, core = mp // 2, mp % 2
    partners = []
    for step in list(range(1, chips)) + [0]:
        for flip in (0, 1):
            if step or flip:
                there = (core + flip) % 2
                partners.append(
                    (
                        ((chip + step) % chips) * 2 + there,
                        ((chip + chips - step) % chips) * 2 + there,
                    )
                )
    ring = [((seq + d) % seq_n, (seq + seq_n - d) % seq_n) for d in range(1, seq_n)]

    def to_mp(src, dst, send, recv, peer):
        return pltpu.make_async_remote_copy(
            src_ref=src,
            dst_ref=dst,
            send_sem=send,
            recv_sem=recv,
            device_id=(sec, seq, peer),
            device_id_type=MESH,
        )

    def to_seq(src, dst, send, recv, peer):
        return pltpu.make_async_remote_copy(
            src_ref=src,
            dst_ref=dst,
            send_sem=send,
            recv_sem=recv,
            device_id=(sec, peer, mp),
            device_id_type=MESH,
        )

    kv_load = pltpu.make_async_copy(kv_hbm, kv_all.at[seq], kv_own_sem)
    kv_load.start()
    q_load = pltpu.make_async_copy(q_hbm, q_buf, q_sem)
    q_load.start()
    w_loads = []
    for n, piece in enumerate([to for to, _ in partners] + [mp]):
        start = pl.multiple_of(piece * cols, cols)
        load = pltpu.make_async_copy(
            w_hbm.at[:, pl.ds(start, cols)], w_buf.at[piece], w_sem.at[n]
        )
        load.start()
        w_loads.append(load)
    x_load = pltpu.make_async_copy(x_hbm, x_buf, x_sem)
    x_load.start()

    barrier = pltpu.get_barrier_semaphore()
    for to, _ in partners:
        pl.semaphore_signal(barrier, inc=1, device_id=(sec, seq, to), device_id_type=MESH)
    for to, _ in ring:
        pl.semaphore_signal(barrier, inc=1, device_id=(sec, to, mp), device_id_type=MESH)
    pl.semaphore_wait(barrier, len(partners) + len(ring))

    kv_copies = []
    for d, (to, _) in enumerate(ring):
        copy = to_seq(kv_hbm, kv_all.at[seq], kv_s.at[d], kv_r.at[d], to)
        copy.start()
        kv_copies.append(copy)
    kv_load.wait()
    for copy in kv_copies:
        copy.wait_recv()
    for t in range(seq_n):
        for h in range(heads):
            at = pl.ds(h * keys + t * own, own)
            k_rows[at, :] = kv_all[t, 0].astype(jnp.float32)
            v_rows[at, :] = kv_all[t, 1].astype(jnp.float32)
    row_head = lax.broadcasted_iota(jnp.int32, (kh, width), 0) // keys
    col_head = lax.broadcasted_iota(jnp.int32, (kh, width), 1) // DH
    diagonal = row_head == col_head
    k_diag = jnp.where(diagonal, k_rows[...], 0.0).astype(jnp.bfloat16)
    v_diag = jnp.where(diagonal, v_rows[...], 0.0).astype(jnp.bfloat16)

    scale = DH ** (-0.5)
    q_load.wait()
    scores = dot(k_diag, q_buf[...], NT) * scale
    key_at = lax.broadcasted_iota(jnp.int32, (keys, rows), 0)
    token_at = lax.broadcasted_iota(jnp.int32, (1, rows), 1) + seq * rows
    allowed = key_at < enc_ref[sec]
    valid = token_at < dec_ref[sec]
    probs = []
    for h in range(heads):
        s = jnp.where(allowed, scores[h * keys : (h + 1) * keys], -1e30)
        e = jnp.where(allowed, jnp.exp(s - jnp.max(s, axis=0, keepdims=True)), 0.0)
        e = e / jnp.sum(e, axis=0, keepdims=True)
        probs.append(jnp.where(valid, e, 0.0))
    prob = jnp.concatenate(probs, axis=0) if heads > 1 else probs[0]
    p_all[mp] = prob.astype(jnp.bfloat16)
    p_copies = []
    for d, (to, _) in enumerate(partners):
        copy = to_mp(p_all.at[mp], p_all.at[mp], p_s.at[d], p_r.at[d], to)
        copy.start()
        p_copies.append(copy)

    vw_copies = []
    for d, (to, _) in enumerate(partners):
        w_loads[d].wait()
        vw_send[to] = dot(v_diag, w_buf[to], NN).astype(jnp.bfloat16)
        copy = to_mp(vw_send.at[to], vw_all.at[mp], vw_s.at[d], vw_r.at[d], to)
        copy.start()
        vw_copies.append(copy)
    w_loads[-1].wait()
    vw_all[mp] = dot(v_diag, w_buf[mp], NN).astype(jnp.bfloat16)

    x_load.wait()
    t_copies = []
    for d, (to, source) in enumerate(partners):
        p_copies[d].wait_recv()
        t_send[source] = dot(p_all[source], x_buf[...], NN).astype(jnp.bfloat16)
        copy = to_mp(t_send.at[source], t_all.at[mp], t_s.at[d], t_r.at[d], source)
        copy.start()
        t_copies.append(copy)
    t_all[mp] = dot(p_all[mp], x_buf[...], NN).astype(jnp.bfloat16)

    gp_copies = []
    for d, (to, source) in enumerate(partners):
        vw_copies[d].wait_recv()
        gp_send[source] = dot(vw_all[source], x_buf[...], NT)
        copy = to_mp(gp_send.at[source], gp_all.at[mp], gp_s.at[d], gp_r.at[d], source)
        copy.start()
        gp_copies.append(copy)
    grad_prob = dot(vw_all[mp], x_buf[...], NT)
    value_part = dot(t_all[mp], w_buf[mp], NT)
    for d, (to, _) in enumerate(partners):
        gp_copies[d].wait_recv()
        grad_prob += gp_all[to]

    grads = []
    for h in range(heads):
        at = slice(h * keys, (h + 1) * keys)
        delta = jnp.sum(prob[at] * grad_prob[at], axis=0, keepdims=True)
        grads.append(prob[at] * (grad_prob[at] - delta))
    grad_score = (jnp.concatenate(grads, axis=0) if heads > 1 else grads[0]).astype(jnp.bfloat16)
    key_part = dot(grad_score, q_buf[...], NN) * scale
    for d, (to, _) in enumerate(partners):
        t_copies[d].wait_recv()
        value_part += dot(t_all[to], w_buf[to], NT)

    def own_head(part):
        part = jnp.where(diagonal, part, 0.0)
        return sum(part[h * keys : (h + 1) * keys] for h in range(heads))

    key_part, value_part = own_head(key_part), own_head(value_part)
    for t in range(seq_n):
        kvg_send[t, pl.ds(0, own), :] = key_part[t * own : (t + 1) * own]
        kvg_send[t, pl.ds(own, own), :] = value_part[t * own : (t + 1) * own]
    kvg_copies = []
    for d, (to, _) in enumerate(ring):
        copy = to_seq(kvg_send.at[to], kvg_all.at[seq], kvg_s.at[d], kvg_r.at[d], to)
        copy.start()
        kvg_copies.append(copy)

    qg_buf[...] = (dot(grad_score, k_diag, TN) * scale).astype(jnp.bfloat16)
    qg_store = pltpu.make_async_copy(qg_buf, qg_hbm, qg_sem)
    qg_store.start()

    total = kvg_send[seq]
    for d, (_, source) in enumerate(ring):
        kvg_copies[d].wait_recv()
        total += kvg_all[source]
    kvg_ref[0] = total[:own].astype(jnp.bfloat16)
    kvg_ref[1] = total[own:].astype(jnp.bfloat16)

    for copy in kv_copies + p_copies + vw_copies + t_copies + gp_copies + kvg_copies:
        copy.wait_send()
    qg_store.wait()


def body(queries, keys_values, out_grad, out_weight, enc_len, dec_len):
    seq_n, mp_n = lax.axis_size("seq"), lax.axis_size("mp")
    rows, width = queries.shape
    cols = out_grad.shape[1]
    own = keys_values.shape[1]
    keys = own * seq_n
    kh = width // DH * keys
    bf16, f32 = jnp.bfloat16, jnp.float32
    any_space = pl.BlockSpec(memory_space=pl.ANY)
    smem = pl.BlockSpec(memory_space=pltpu.SMEM)
    dma = pltpu.SemaphoreType.DMA
    return pl.pallas_call(
        functools.partial(kernel, seq_n, mp_n),
        out_shape=(
            jax.ShapeDtypeStruct((rows, width), bf16),
            jax.ShapeDtypeStruct((2, own, width), bf16),
        ),
        in_specs=[smem, smem, any_space, any_space, any_space, any_space],
        out_specs=(any_space, pl.BlockSpec(memory_space=pltpu.VMEM)),
        scratch_shapes=[
            pltpu.VMEM((rows, width), bf16),
            pltpu.VMEM((rows, cols), bf16),
            pltpu.VMEM((mp_n, width, cols), bf16),
            pltpu.VMEM((seq_n, 2, own, width), bf16),
            pltpu.VMEM((kh, width), f32),
            pltpu.VMEM((kh, width), f32),
            pltpu.VMEM((mp_n, kh, rows), bf16),
            pltpu.VMEM((mp_n, kh, cols), bf16),
            pltpu.VMEM((mp_n, kh, cols), bf16),
            pltpu.VMEM((mp_n, kh, rows), f32),
            pltpu.VMEM((mp_n, kh, rows), f32),
            pltpu.VMEM((mp_n, kh, cols), bf16),
            pltpu.VMEM((mp_n, kh, cols), bf16),
            pltpu.VMEM((seq_n, 2 * own, width), f32),
            pltpu.VMEM((seq_n, 2 * own, width), f32),
            pltpu.VMEM((rows, width), bf16),
            dma,
            dma,
            dma((mp_n,)),
            dma,
            dma,
            dma((seq_n,)),
            dma((seq_n,)),
            dma((mp_n,)),
            dma((mp_n,)),
            dma((mp_n,)),
            dma((mp_n,)),
            dma((mp_n,)),
            dma((mp_n,)),
            dma((mp_n,)),
            dma((mp_n,)),
            dma((seq_n,)),
            dma((seq_n,)),
        ],
        compiler_params=pltpu.CompilerParams(
            collective_id=0, has_side_effects=True, vmem_limit_bytes=48 * 2**20
        ),
        name="cross_attention_backward",
    )(enc_len, dec_len, queries, keys_values, out_grad, out_weight)


def solution(mesh):
    assert mesh.shape["sec"] == SEQS
    placed = (
        P(("sec", "seq"), "mp"),
        P(None, ("sec", "seq"), "mp"),
        P(("sec", "seq"), "mp"),
        P("mp", None),
        P(),
        P(),
    )
    return jax.shard_map(
        body,
        mesh=mesh,
        in_specs=placed,
        out_specs=(P(("sec", "seq"), "mp"), P(None, ("sec", "seq"), "mp")),
        check_vma=False,
    )
```

```python
import functools

import jax
import jax.numpy as jnp
from jax import lax
from jax.experimental import pallas as pl
from jax.experimental.pallas import tpu as pltpu
from jax.sharding import PartitionSpec as P

DH = 256
SEQS = 2
MESH = pl.DeviceIdType.MESH
NN = (((1,), (0,)), ((), ()))
NT = (((1,), (1,)), ((), ()))
TN = (((0,), (0,)), ((), ()))


def dot(a, b, dims):
    return lax.dot_general(a, b, dims, preferred_element_type=jnp.float32)


def kernel(
    seq_n,
    mp_n,
    enc_hbm,
    dec_hbm,
    q_hbm,
    kv_hbm,
    x_hbm,
    w_hbm,
    qg_hbm,
    kvg_ref,
    enc_buf,
    dec_buf,
    q_buf,
    x_buf,
    w_buf,
    kv_all,
    k_rows,
    v_rows,
    p_all,
    vw_send,
    vw_all,
    gp_send,
    gp_all,
    t_send,
    t_all,
    kvg_send,
    kvg_all,
    qg_buf,
    len_sem,
    qg_sem,
    q_sem,
    x_sem,
    w_sem,
    kv_own_sem,
    kv_s,
    kv_r,
    p_s,
    p_r,
    vw_s,
    vw_r,
    gp_s,
    gp_r,
    t_s,
    t_r,
    kvg_s,
    kvg_r,
):
    sec = lax.axis_index("sec")
    seq = lax.axis_index("seq")
    mp = lax.axis_index("mp")
    rows, width = q_buf.shape
    cols = x_buf.shape[1]
    own = kv_hbm.shape[1]
    heads = width // DH
    keys = own * seq_n
    kh = heads * keys

    chips = mp_n // 2
    chip, core = mp // 2, mp % 2
    partners = []
    for step in list(range(1, chips)) + [0]:
        for flip in (0, 1):
            if step or flip:
                there = (core + flip) % 2
                partners.append(
                    (
                        ((chip + step) % chips) * 2 + there,
                        ((chip + chips - step) % chips) * 2 + there,
                    )
                )
    ring = [((seq + d) % seq_n, (seq + seq_n - d) % seq_n) for d in range(1, seq_n)]

    def to_mp(src, dst, send, recv, peer):
        return pltpu.make_async_remote_copy(
            src_ref=src,
            dst_ref=dst,
            send_sem=send,
            recv_sem=recv,
            device_id=(sec, seq, peer),
            device_id_type=MESH,
        )

    def to_seq(src, dst, send, recv, peer):
        return pltpu.make_async_remote_copy(
            src_ref=src,
            dst_ref=dst,
            send_sem=send,
            recv_sem=recv,
            device_id=(sec, peer, mp),
            device_id_type=MESH,
        )

    barrier = pltpu.get_barrier_semaphore()
    for to, _ in partners:
        pl.semaphore_signal(barrier, inc=1, device_id=(sec, seq, to), device_id_type=MESH)
    for to, _ in ring:
        pl.semaphore_signal(barrier, inc=1, device_id=(sec, to, mp), device_id_type=MESH)

    kv_load = pltpu.make_async_copy(kv_hbm, kv_all.at[seq], kv_own_sem)
    kv_load.start()
    q_load = pltpu.make_async_copy(q_hbm, q_buf, q_sem)
    q_load.start()
    w_loads = []
    for n, piece in enumerate([to for to, _ in partners] + [mp]):
        start = pl.multiple_of(piece * cols, cols)
        load = pltpu.make_async_copy(
            w_hbm.at[:, pl.ds(start, cols)], w_buf.at[piece], w_sem.at[n]
        )
        load.start()
        w_loads.append(load)
    x_load = pltpu.make_async_copy(x_hbm, x_buf, x_sem)
    x_load.start()
    enc_load = pltpu.make_async_copy(enc_hbm, enc_buf, len_sem.at[0])
    enc_load.start()
    dec_load = pltpu.make_async_copy(dec_hbm, dec_buf, len_sem.at[1])
    dec_load.start()

    pl.semaphore_wait(barrier, len(partners) + len(ring))

    kv_copies = []
    for d, (to, _) in enumerate(ring):
        copy = to_seq(kv_hbm, kv_all.at[seq], kv_s.at[d], kv_r.at[d], to)
        copy.start()
        kv_copies.append(copy)
    kv_load.wait()
    for copy in kv_copies:
        copy.wait_recv()
    for t in range(seq_n):
        for h in range(heads):
            at = pl.ds(h * keys + t * own, own)
            k_rows[at, :] = kv_all[t, 0].astype(jnp.float32)
            v_rows[at, :] = kv_all[t, 1].astype(jnp.float32)
    row_head = lax.broadcasted_iota(jnp.int32, (kh, width), 0) // keys
    col_head = lax.broadcasted_iota(jnp.int32, (kh, width), 1) // DH
    diagonal = row_head == col_head
    k_diag = jnp.where(diagonal, k_rows[...], 0.0).astype(jnp.bfloat16)
    v_diag = jnp.where(diagonal, v_rows[...], 0.0).astype(jnp.bfloat16)

    scale = DH ** (-0.5)
    q_load.wait()
    scores = dot(k_diag, q_buf[...], NT) * scale
    key_at = lax.broadcasted_iota(jnp.int32, (keys, rows), 0)
    token_at = lax.broadcasted_iota(jnp.int32, (1, rows), 1) + seq * rows
    enc_load.wait()
    dec_load.wait()
    allowed = key_at < enc_buf[sec]
    valid = token_at < dec_buf[sec]
    probs = []
    for h in range(heads):
        s = jnp.where(allowed, scores[h * keys : (h + 1) * keys], -1e30)
        e = jnp.where(allowed, jnp.exp(s - jnp.max(s, axis=0, keepdims=True)), 0.0)
        e = e / jnp.sum(e, axis=0, keepdims=True)
        probs.append(jnp.where(valid, e, 0.0))
    prob = jnp.concatenate(probs, axis=0) if heads > 1 else probs[0]
    p_all[mp] = prob.astype(jnp.bfloat16)
    p_copies = []
    for d, (to, _) in enumerate(partners):
        copy = to_mp(p_all.at[mp], p_all.at[mp], p_s.at[d], p_r.at[d], to)
        copy.start()
        p_copies.append(copy)

    vw_copies = []
    for d, (to, _) in enumerate(partners):
        w_loads[d].wait()
        vw_send[to] = dot(v_diag, w_buf[to], NN).astype(jnp.bfloat16)
        copy = to_mp(vw_send.at[to], vw_all.at[mp], vw_s.at[d], vw_r.at[d], to)
        copy.start()
        vw_copies.append(copy)
    w_loads[-1].wait()
    vw_all[mp] = dot(v_diag, w_buf[mp], NN).astype(jnp.bfloat16)

    x_load.wait()
    for copy in p_copies:
        copy.wait_recv()
    t_rows = dot(p_all[...].reshape(mp_n * kh, rows), x_buf[...], NN)
    t_send[...] = t_rows.astype(jnp.bfloat16).reshape(mp_n, kh, cols)
    t_copies = []
    for d, (_, source) in enumerate(partners):
        copy = to_mp(t_send.at[source], t_all.at[mp], t_s.at[d], t_r.at[d], source)
        copy.start()
        t_copies.append(copy)

    for copy in vw_copies:
        copy.wait_recv()
    gp_rows = dot(vw_all[...].reshape(mp_n * kh, cols), x_buf[...], NT)
    gp_send[...] = gp_rows.reshape(mp_n, kh, rows)
    gp_copies = []
    for d, (_, source) in enumerate(partners):
        copy = to_mp(gp_send.at[source], gp_all.at[mp], gp_s.at[d], gp_r.at[d], source)
        copy.start()
        gp_copies.append(copy)
    grad_prob = gp_send[mp]
    value_part = dot(t_send[mp], w_buf[mp], NT)
    for d, (to, _) in enumerate(partners):
        gp_copies[d].wait_recv()
        grad_prob += gp_all[to]

    grads = []
    for h in range(heads):
        at = slice(h * keys, (h + 1) * keys)
        delta = jnp.sum(prob[at] * grad_prob[at], axis=0, keepdims=True)
        grads.append(prob[at] * (grad_prob[at] - delta))
    grad_score = (jnp.concatenate(grads, axis=0) if heads > 1 else grads[0]).astype(jnp.bfloat16)
    key_part = dot(grad_score, q_buf[...], NN) * scale
    for d, (to, _) in enumerate(partners):
        t_copies[d].wait_recv()
        value_part += dot(t_all[to], w_buf[to], NT)

    def own_head(part):
        part = jnp.where(diagonal, part, 0.0)
        return sum(part[h * keys : (h + 1) * keys] for h in range(heads))

    key_part, value_part = own_head(key_part), own_head(value_part)
    for t in range(seq_n):
        kvg_send[t, pl.ds(0, own), :] = key_part[t * own : (t + 1) * own]
        kvg_send[t, pl.ds(own, own), :] = value_part[t * own : (t + 1) * own]
    kvg_copies = []
    for d, (to, _) in enumerate(ring):
        copy = to_seq(kvg_send.at[to], kvg_all.at[seq], kvg_s.at[d], kvg_r.at[d], to)
        copy.start()
        kvg_copies.append(copy)

    qg_buf[...] = (dot(grad_score, k_diag, TN) * scale).astype(jnp.bfloat16)
    qg_store = pltpu.make_async_copy(qg_buf, qg_hbm, qg_sem)
    qg_store.start()

    total = kvg_send[seq]
    for d, (_, source) in enumerate(ring):
        kvg_copies[d].wait_recv()
        total += kvg_all[source]
    kvg_ref[0] = total[:own].astype(jnp.bfloat16)
    kvg_ref[1] = total[own:].astype(jnp.bfloat16)

    for copy in kv_copies + p_copies + vw_copies + t_copies + gp_copies + kvg_copies:
        copy.wait_send()
    qg_store.wait()


def body(queries, keys_values, out_grad, out_weight, enc_len, dec_len):
    seq_n, mp_n = lax.axis_size("seq"), lax.axis_size("mp")
    rows, width = queries.shape
    cols = out_grad.shape[1]
    own = keys_values.shape[1]
    keys = own * seq_n
    kh = width // DH * keys
    bf16, f32 = jnp.bfloat16, jnp.float32
    hbm = pl.BlockSpec(memory_space=pltpu.HBM)
    vmem = pl.BlockSpec(memory_space=pltpu.VMEM)
    dma = pltpu.SemaphoreType.DMA
    return pl.pallas_call(
        functools.partial(kernel, seq_n, mp_n),
        out_shape=(
            jax.ShapeDtypeStruct((rows, width), bf16),
            jax.ShapeDtypeStruct((2, own, width), bf16),
        ),
        in_specs=[hbm] * 6,
        out_specs=(hbm, vmem),
        scratch_shapes=[
            pltpu.SMEM((SEQS,), jnp.int32),
            pltpu.SMEM((SEQS,), jnp.int32),
            pltpu.VMEM((rows, width), bf16),
            pltpu.VMEM((rows, cols), bf16),
            pltpu.VMEM((mp_n, width, cols), bf16),
            pltpu.VMEM((seq_n, 2, own, width), bf16),
            pltpu.VMEM((kh, width), f32),
            pltpu.VMEM((kh, width), f32),
            pltpu.VMEM((mp_n, kh, rows), bf16),
            pltpu.VMEM((mp_n, kh, cols), bf16),
            pltpu.VMEM((mp_n, kh, cols), bf16),
            pltpu.VMEM((mp_n, kh, rows), f32),
            pltpu.VMEM((mp_n, kh, rows), f32),
            pltpu.VMEM((mp_n, kh, cols), bf16),
            pltpu.VMEM((mp_n, kh, cols), bf16),
            pltpu.VMEM((seq_n, 2 * own, width), f32),
            pltpu.VMEM((seq_n, 2 * own, width), f32),
            pltpu.VMEM((rows, width), bf16),
            dma((2,)),
            dma,
            dma,
            dma,
            dma((mp_n,)),
            dma,
            dma((seq_n,)),
            dma((seq_n,)),
            dma((mp_n,)),
            dma((mp_n,)),
            dma((mp_n,)),
            dma((mp_n,)),
            dma((mp_n,)),
            dma((mp_n,)),
            dma((mp_n,)),
            dma((mp_n,)),
            dma((seq_n,)),
            dma((seq_n,)),
        ],
        compiler_params=pltpu.CompilerParams(
            collective_id=0, has_side_effects=True, vmem_limit_bytes=63 * 2**20
        ),
        name="cross_attention_backward",
    )(enc_len, dec_len, queries, keys_values, out_grad, out_weight)


def solution(mesh):
    assert mesh.shape["sec"] == SEQS
    placed = (
        P(("sec", "seq"), "mp"),
        P(None, ("sec", "seq"), "mp"),
        P(("sec", "seq"), "mp"),
        P("mp", None),
        P(),
        P(),
    )
    return jax.shard_map(
        body,
        mesh=mesh,
        in_specs=placed,
        out_specs=(P(("sec", "seq"), "mp"), P(None, ("sec", "seq"), "mp")),
        check_vma=False,
    )
```

```python
import functools

import jax
import jax.numpy as jnp
from jax import lax
from jax.experimental import pallas as pl
from jax.experimental.pallas import tpu as pltpu
from jax.sharding import PartitionSpec as P

DH = 256
SEQS = 2
CHUNK = 256
MESH = pl.DeviceIdType.MESH
NN = (((1,), (0,)), ((), ()))
NT = (((1,), (1,)), ((), ()))
TN = (((0,), (0,)), ((), ()))


def dot(a, b, dims):
    return lax.dot_general(a, b, dims, preferred_element_type=jnp.float32)


def kernel(
    seq_n,
    mp_n,
    enc_hbm,
    dec_hbm,
    q_hbm,
    kv_hbm,
    x_hbm,
    w_hbm,
    qg_ref,
    kvg_ref,
    enc_buf,
    dec_buf,
    q_buf,
    x_all,
    w_buf,
    kv_all,
    k_rows,
    v_rows,
    g_sum,
    kvg_send,
    kvg_all,
    len_sem,
    q_sem,
    x_sem,
    w_sem,
    kv_own_sem,
    kv_s,
    kv_r,
    pair_s,
    pair_r,
    far_s,
    far_r,
    pass_s,
    pass_r,
    kvg_s,
    kvg_r,
):
    sec = lax.axis_index("sec")
    seq = lax.axis_index("seq")
    mp = lax.axis_index("mp")
    rows, width = q_buf.shape
    chunks = x_all.shape[1]
    cols = chunks * CHUNK
    own = kv_hbm.shape[1]
    heads = width // DH
    keys = own * seq_n
    kh = heads * keys

    chips = mp_n // 2
    chip, core = mp // 2, mp % 2
    pair = chip * 2 + 1 - core
    far = [
        (((chip + d) % chips) * 2 + core, ((chip + chips - d) % chips) * 2 + core)
        for d in range(1, chips)
    ]
    ring = [((seq + d) % seq_n, (seq + seq_n - d) % seq_n) for d in range(1, seq_n)]

    def to_mp(src, dst, send, recv, peer):
        return pltpu.make_async_remote_copy(
            src_ref=src,
            dst_ref=dst,
            send_sem=send,
            recv_sem=recv,
            device_id=(sec, seq, peer),
            device_id_type=MESH,
        )

    def to_seq(src, dst, send, recv, peer):
        return pltpu.make_async_remote_copy(
            src_ref=src,
            dst_ref=dst,
            send_sem=send,
            recv_sem=recv,
            device_id=(sec, peer, mp),
            device_id_type=MESH,
        )

    barrier = pltpu.get_barrier_semaphore()
    for to in [pair] + [to for to, _ in far]:
        pl.semaphore_signal(barrier, inc=1, device_id=(sec, seq, to), device_id_type=MESH)
    for to, _ in ring:
        pl.semaphore_signal(barrier, inc=1, device_id=(sec, to, mp), device_id_type=MESH)

    kv_load = pltpu.make_async_copy(kv_hbm, kv_all.at[seq], kv_own_sem)
    kv_load.start()
    q_load = pltpu.make_async_copy(q_hbm, q_buf, q_sem)
    q_load.start()
    enc_load = pltpu.make_async_copy(enc_hbm, enc_buf, len_sem.at[0])
    enc_load.start()
    dec_load = pltpu.make_async_copy(dec_hbm, dec_buf, len_sem.at[1])
    dec_load.start()
    x_loads = []
    for c in range(chunks):
        load = pltpu.make_async_copy(
            x_hbm.at[:, pl.ds(c * CHUNK, CHUNK)], x_all.at[mp, c], x_sem.at[c]
        )
        load.start()
        x_loads.append(load)
    order = [mp, pair] + [source for _, source in far]
    for _, source in far:
        order.append((source // 2) * 2 + 1 - core)
    w_loads = []
    for n, piece in enumerate(order):
        start = pl.multiple_of(piece * cols, cols)
        load = pltpu.make_async_copy(
            w_hbm.at[:, pl.ds(start, cols)], w_buf.at[piece], w_sem.at[n]
        )
        load.start()
        w_loads.append(load)

    pl.semaphore_wait(barrier, 1 + len(far) + len(ring))

    kv_copies = []
    for d, (to, _) in enumerate(ring):
        copy = to_seq(kv_hbm, kv_all.at[seq], kv_s.at[d], kv_r.at[d], to)
        copy.start()
        kv_copies.append(copy)
    far_copies = {}
    pair_copies = []
    for c in range(chunks):
        part = x_hbm.at[:, pl.ds(c * CHUNK, CHUNK)]
        for d, (to, _) in enumerate(far):
            copy = to_mp(part, x_all.at[mp, c], far_s.at[d, c], far_r.at[d, c], to)
            copy.start()
            far_copies[d, c] = copy
        copy = to_mp(part, x_all.at[mp, c], pair_s.at[c], pair_r.at[c], pair)
        copy.start()
        pair_copies.append(copy)

    def part_of(source, c):
        return dot(x_all[source, c], w_buf[source, :, c * CHUNK : (c + 1) * CHUNK], NT)

    for load in x_loads:
        load.wait()
    w_loads[0].wait()
    total = part_of(mp, 0)
    for c in range(1, chunks):
        total += part_of(mp, c)
    g_sum[...] = total

    for copy in pair_copies:
        copy.wait_recv()
    w_loads[1].wait()
    total = g_sum[...]
    for c in range(chunks):
        total += part_of(pair, c)
    g_sum[...] = total

    kv_load.wait()
    for copy in kv_copies:
        copy.wait_recv()
    for t in range(seq_n):
        for h in range(heads):
            at = pl.ds(h * keys + t * own, own)
            k_rows[at, :] = kv_all[t, 0].astype(jnp.float32)
            v_rows[at, :] = kv_all[t, 1].astype(jnp.float32)
    row_head = lax.broadcasted_iota(jnp.int32, (kh, width), 0) // keys
    col_head = lax.broadcasted_iota(jnp.int32, (kh, width), 1) // DH
    diagonal = row_head == col_head
    k_diag = jnp.where(diagonal, k_rows[...], 0.0).astype(jnp.bfloat16)
    v_diag = jnp.where(diagonal, v_rows[...], 0.0).astype(jnp.bfloat16)

    scale = DH ** (-0.5)
    q_load.wait()
    scores = dot(k_diag, q_buf[...], NT) * scale
    key_at = lax.broadcasted_iota(jnp.int32, (keys, rows), 0)
    token_at = lax.broadcasted_iota(jnp.int32, (1, rows), 1) + seq * rows
    enc_load.wait()
    dec_load.wait()
    allowed = key_at < enc_buf[sec]
    valid = token_at < dec_buf[sec]
    probs = []
    for h in range(heads):
        s = jnp.where(allowed, scores[h * keys : (h + 1) * keys], -1e30)
        e = jnp.where(allowed, jnp.exp(s - jnp.max(s, axis=0, keepdims=True)), 0.0)
        e = e / jnp.sum(e, axis=0, keepdims=True)
        probs.append(jnp.where(valid, e, 0.0))
    prob = jnp.concatenate(probs, axis=0) if heads > 1 else probs[0]
    prob_bf16 = prob.astype(jnp.bfloat16)

    for load in w_loads[2:]:
        load.wait()
    pass_copies = {}
    for c in range(chunks + 1):
        if c < chunks:
            for d, (_, source) in enumerate(far):
                far_copies[d, c].wait_recv()
                slot = x_all.at[source, c]
                copy = to_mp(slot, slot, pass_s.at[d, c], pass_r.at[d, c], pair)
                copy.start()
                pass_copies[d, c] = copy
        total = g_sum[...]
        if c < chunks:
            for _, source in far:
                total += part_of(source, c)
        if c > 0:
            for d, (_, source) in enumerate(far):
                pass_copies[d, c - 1].wait_recv()
                total += part_of((source // 2) * 2 + 1 - core, c - 1)
        if c < chunks:
            g_sum[...] = total
    g = total.astype(jnp.bfloat16)

    value_part = dot(prob_bf16, g, NN)
    grad_prob = dot(v_diag, g, NT)
    grads = []
    for h in range(heads):
        at = slice(h * keys, (h + 1) * keys)
        delta = jnp.sum(prob[at] * grad_prob[at], axis=0, keepdims=True)
        grads.append(prob[at] * (grad_prob[at] - delta))
    grad_score = (jnp.concatenate(grads, axis=0) if heads > 1 else grads[0]).astype(jnp.bfloat16)
    key_part = dot(grad_score, q_buf[...], NN) * scale

    def own_head(part):
        part = jnp.where(diagonal, part, 0.0)
        return sum(part[h * keys : (h + 1) * keys] for h in range(heads))

    key_part, value_part = own_head(key_part), own_head(value_part)
    for t in range(seq_n):
        kvg_send[t, pl.ds(0, own), :] = key_part[t * own : (t + 1) * own]
        kvg_send[t, pl.ds(own, own), :] = value_part[t * own : (t + 1) * own]
    kvg_copies = []
    for d, (to, _) in enumerate(ring):
        copy = to_seq(kvg_send.at[to], kvg_all.at[seq], kvg_s.at[d], kvg_r.at[d], to)
        copy.start()
        kvg_copies.append(copy)

    qg_ref[...] = (dot(grad_score, k_diag, TN) * scale).astype(jnp.bfloat16)

    total = kvg_send[seq]
    for d, (_, source) in enumerate(ring):
        kvg_copies[d].wait_recv()
        total += kvg_all[source]
    kvg_ref[0] = total[:own].astype(jnp.bfloat16)
    kvg_ref[1] = total[own:].astype(jnp.bfloat16)

    sent = kv_copies + pair_copies + kvg_copies
    for copy in sent + list(far_copies.values()) + list(pass_copies.values()):
        copy.wait_send()


def store_kernel(qg_ref, kvg_ref, qg_hbm, kvg_hbm, sem):
    copies = [
        pltpu.make_async_copy(qg_ref, qg_hbm, sem.at[0]),
        pltpu.make_async_copy(kvg_ref, kvg_hbm, sem.at[1]),
    ]
    for copy in copies:
        copy.start()
    for copy in copies:
        copy.wait()


def body(queries, keys_values, out_grad, out_weight, enc_len, dec_len):
    seq_n, mp_n = lax.axis_size("seq"), lax.axis_size("mp")
    rows, width = queries.shape
    cols = out_grad.shape[1]
    chunks = cols // CHUNK
    own = keys_values.shape[1]
    keys = own * seq_n
    kh = width // DH * keys
    far_n = max(mp_n // 2 - 1, 1)
    bf16, f32 = jnp.bfloat16, jnp.float32
    hbm = pl.BlockSpec(memory_space=pltpu.HBM)
    vmem = pl.BlockSpec(memory_space=pltpu.VMEM)
    dma = pltpu.SemaphoreType.DMA
    operands = [
        pltpu.with_memory_space_constraint(a, pltpu.HBM)
        for a in (enc_len, dec_len, queries, keys_values, out_grad, out_weight)
    ]
    results = pl.pallas_call(
        functools.partial(kernel, seq_n, mp_n),
        out_shape=(
            pltpu.VMEM((rows, width), bf16),
            pltpu.VMEM((2, own, width), bf16),
        ),
        in_specs=[hbm] * 6,
        out_specs=(vmem, vmem),
        scratch_shapes=[
            pltpu.SMEM((SEQS,), jnp.int32),
            pltpu.SMEM((SEQS,), jnp.int32),
            pltpu.VMEM((rows, width), bf16),
            pltpu.VMEM((mp_n, chunks, rows, CHUNK), bf16),
            pltpu.VMEM((mp_n, width, cols), bf16),
            pltpu.VMEM((seq_n, 2, own, width), bf16),
            pltpu.VMEM((kh, width), f32),
            pltpu.VMEM((kh, width), f32),
            pltpu.VMEM((rows, width), f32),
            pltpu.VMEM((seq_n, 2 * own, width), f32),
            pltpu.VMEM((seq_n, 2 * own, width), f32),
            dma((2,)),
            dma,
            dma((chunks,)),
            dma((mp_n,)),
            dma,
            dma((seq_n,)),
            dma((seq_n,)),
            dma((chunks,)),
            dma((chunks,)),
            dma((far_n, chunks)),
            dma((far_n, chunks)),
            dma((far_n, chunks)),
            dma((far_n, chunks)),
            dma((seq_n,)),
            dma((seq_n,)),
        ],
        compiler_params=pltpu.CompilerParams(
            collective_id=0, has_side_effects=True, vmem_limit_bytes=48 * 2**20
        ),
        name="cross_attention_backward",
    )(*operands)
    return pl.pallas_call(
        store_kernel,
        out_shape=(
            jax.ShapeDtypeStruct((rows, width), bf16),
            jax.ShapeDtypeStruct((2, own, width), bf16),
        ),
        in_specs=[vmem, vmem],
        out_specs=(hbm, hbm),
        scratch_shapes=[dma((2,))],
        name="store_results",
    )(*results)


def solution(mesh):
    assert mesh.shape["sec"] == SEQS
    placed = (
        P(("sec", "seq"), "mp"),
        P(None, ("sec", "seq"), "mp"),
        P(("sec", "seq"), "mp"),
        P("mp", None),
        P(),
        P(),
    )
    return jax.shard_map(
        body,
        mesh=mesh,
        in_specs=placed,
        out_specs=(P(("sec", "seq"), "mp"), P(None, ("sec", "seq"), "mp")),
        check_vma=False,
    )
```

```python
import functools

import jax
import jax.numpy as jnp
from jax import lax
from jax.experimental import pallas as pl
from jax.experimental.pallas import tpu as pltpu
from jax.sharding import PartitionSpec as P

DH = 256
SEQS = 2
LANES = 128
MESH = pl.DeviceIdType.MESH
NN = (((1,), (0,)), ((), ()))
NT = (((1,), (1,)), ((), ()))
TN = (((0,), (0,)), ((), ()))


def dot(a, b, dims):
    return lax.dot_general(a, b, dims, preferred_element_type=jnp.float32)


def pieces_of(cols):
    edges = list(range(0, cols, max(cols // 4, LANES))) + [cols]
    middle = (edges[-2] + cols) // 2
    if middle % LANES == 0 and middle > edges[-2]:
        edges.insert(-1, middle)
    return list(zip(edges[:-1], edges[1:]))


def kernel(
    seq_n,
    mp_n,
    enc_hbm,
    dec_hbm,
    q_hbm,
    kv_hbm,
    x_hbm,
    w_hbm,
    qg_ref,
    kvg_ref,
    enc_buf,
    dec_buf,
    q_buf,
    x_all,
    w_buf,
    kv_all,
    k_rows,
    v_rows,
    g_sum,
    kvg_send,
    kvg_all,
    len_sem,
    q_sem,
    x_sem,
    w_sem,
    kv_own_sem,
    kv_s,
    kv_r,
    pair_s,
    pair_r,
    far_s,
    far_r,
    cross_s,
    cross_r,
    pass_s,
    pass_r,
    kvg_s,
    kvg_r,
):
    sec = lax.axis_index("sec")
    seq = lax.axis_index("seq")
    mp = lax.axis_index("mp")
    rows, width = q_buf.shape
    cols = x_all.shape[2]
    pieces = pieces_of(cols)
    last = len(pieces) - 1
    own = kv_hbm.shape[1]
    heads = width // DH
    keys = own * seq_n
    kh = heads * keys

    chips = mp_n // 2
    chip, core = mp // 2, mp % 2
    pair = chip * 2 + 1 - core
    far = [
        (((chip + d) % chips) * 2 + core, ((chip + chips - d) % chips) * 2 + core)
        for d in range(1, chips)
    ]
    cross = [(to + 1 - 2 * core, source + 1 - 2 * core) for to, source in far]
    ring = [((seq + d) % seq_n, (seq + seq_n - d) % seq_n) for d in range(1, seq_n)]

    def to_mp(src, dst, send, recv, peer):
        return pltpu.make_async_remote_copy(
            src_ref=src,
            dst_ref=dst,
            send_sem=send,
            recv_sem=recv,
            device_id=(sec, seq, peer),
            device_id_type=MESH,
        )

    def to_seq(src, dst, send, recv, peer):
        return pltpu.make_async_remote_copy(
            src_ref=src,
            dst_ref=dst,
            send_sem=send,
            recv_sem=recv,
            device_id=(sec, peer, mp),
            device_id_type=MESH,
        )

    barrier = pltpu.get_barrier_semaphore()
    for to in [pair] + [to for to, _ in far + cross]:
        pl.semaphore_signal(barrier, inc=1, device_id=(sec, seq, to), device_id_type=MESH)
    for to, _ in ring:
        pl.semaphore_signal(barrier, inc=1, device_id=(sec, to, mp), device_id_type=MESH)

    pl.semaphore_wait(barrier, 1 + 2 * len(far) + len(ring))

    kv_copies = []
    for d, (to, _) in enumerate(ring):
        copy = to_seq(kv_hbm, kv_all.at[seq], kv_s.at[d], kv_r.at[d], to)
        copy.start()
        kv_copies.append(copy)
    far_copies = {}
    for c, (start, end) in enumerate(pieces):
        at = (slice(None), pl.ds(start, end - start))
        for d, (to, _) in enumerate(far):
            copy = to_mp(
                x_hbm.at[at], x_all.at[(mp,) + at], far_s.at[d, c], far_r.at[d, c], to
            )
            copy.start()
            far_copies[d, c] = copy
        if c == 0:
            pair_copy = to_mp(x_hbm, x_all.at[mp], pair_s, pair_r, pair)
            pair_copy.start()
    cross_copies = []
    for d, (to, _) in enumerate(cross):
        copy = to_mp(x_hbm.at[at], x_all.at[(mp,) + at], cross_s.at[d], cross_r.at[d], to)
        copy.start()
        cross_copies.append(copy)

    kv_load = pltpu.make_async_copy(kv_hbm, kv_all.at[seq], kv_own_sem)
    kv_load.start()
    q_load = pltpu.make_async_copy(q_hbm, q_buf, q_sem)
    q_load.start()
    enc_load = pltpu.make_async_copy(enc_hbm, enc_buf, len_sem.at[0])
    enc_load.start()
    dec_load = pltpu.make_async_copy(dec_hbm, dec_buf, len_sem.at[1])
    dec_load.start()
    x_load = pltpu.make_async_copy(x_hbm, x_all.at[mp], x_sem)
    x_load.start()
    order = [mp, pair] + [source for _, source in far + cross]
    w_loads = []
    for n, piece in enumerate(order):
        start = pl.multiple_of(piece * cols, cols)
        load = pltpu.make_async_copy(
            w_hbm.at[:, pl.ds(start, cols)], w_buf.at[piece], w_sem.at[n]
        )
        load.start()
        w_loads.append(load)

    def part_of(source, piece):
        at = slice(*piece)
        return dot(x_all[source, :, at], w_buf[source, :, at], NT)

    x_load.wait()
    w_loads[0].wait()
    g_sum[...] = part_of(mp, (0, cols))
    pair_copy.wait_recv()
    w_loads[1].wait()
    g_sum[...] += part_of(pair, (0, cols))

    kv_load.wait()
    for copy in kv_copies:
        copy.wait_recv()
    for t in range(seq_n):
        for h in range(heads):
            at = pl.ds(h * keys + t * own, own)
            k_rows[at, :] = kv_all[t, 0].astype(jnp.float32)
            v_rows[at, :] = kv_all[t, 1].astype(jnp.float32)
    row_head = lax.broadcasted_iota(jnp.int32, (kh, width), 0) // keys
    col_head = lax.broadcasted_iota(jnp.int32, (kh, width), 1) // DH
    diagonal = row_head == col_head
    k_diag = jnp.where(diagonal, k_rows[...], 0.0).astype(jnp.bfloat16)
    v_diag = jnp.where(diagonal, v_rows[...], 0.0).astype(jnp.bfloat16)

    scale = DH ** (-0.5)
    q_load.wait()
    scores = dot(k_diag, q_buf[...], NT) * scale
    key_at = lax.broadcasted_iota(jnp.int32, (keys, rows), 0)
    token_at = lax.broadcasted_iota(jnp.int32, (1, rows), 1) + seq * rows
    enc_load.wait()
    dec_load.wait()
    allowed = key_at < enc_buf[sec]
    valid = token_at < dec_buf[sec]
    probs = []
    for h in range(heads):
        s = jnp.where(allowed, scores[h * keys : (h + 1) * keys], -1e30)
        e = jnp.where(allowed, jnp.exp(s - jnp.max(s, axis=0, keepdims=True)), 0.0)
        e = e / jnp.sum(e, axis=0, keepdims=True)
        probs.append(jnp.where(valid, e, 0.0))
    prob = jnp.concatenate(probs, axis=0) if heads > 1 else probs[0]
    prob_bf16 = prob.astype(jnp.bfloat16)

    for load in w_loads[2:]:
        load.wait()
    pass_copies = {}
    for c, piece in enumerate(pieces):
        for d, (_, source) in enumerate(far):
            far_copies[d, c].wait_recv()
            if c < last:
                slot = x_all.at[source, :, pl.ds(piece[0], piece[1] - piece[0])]
                copy = to_mp(slot, slot, pass_s.at[d, c], pass_r.at[d, c], pair)
                copy.start()
                pass_copies[d, c] = copy
        total = g_sum[...]
        for _, source in far:
            total += part_of(source, piece)
        if c > 0:
            for d, (_, source) in enumerate(cross):
                pass_copies[d, c - 1].wait_recv()
                total += part_of(source, pieces[c - 1])
        if c < last:
            g_sum[...] = total
    for d, (_, source) in enumerate(cross):
        cross_copies[d].wait_recv()
        total += part_of(source, pieces[last])
    g = total.astype(jnp.bfloat16)

    value_part = dot(prob_bf16, g, NN)
    grad_prob = dot(v_diag, g, NT)
    grads = []
    for h in range(heads):
        at = slice(h * keys, (h + 1) * keys)
        delta = jnp.sum(prob[at] * grad_prob[at], axis=0, keepdims=True)
        grads.append(prob[at] * (grad_prob[at] - delta))
    grad_score = (jnp.concatenate(grads, axis=0) if heads > 1 else grads[0]).astype(jnp.bfloat16)
    key_part = dot(grad_score, q_buf[...], NN) * scale

    def own_head(part):
        part = jnp.where(diagonal, part, 0.0)
        return sum(part[h * keys : (h + 1) * keys] for h in range(heads))

    key_part, value_part = own_head(key_part), own_head(value_part)
    for t in range(seq_n):
        kvg_send[t, pl.ds(0, own), :] = key_part[t * own : (t + 1) * own]
        kvg_send[t, pl.ds(own, own), :] = value_part[t * own : (t + 1) * own]
    kvg_copies = []
    for d, (to, _) in enumerate(ring):
        copy = to_seq(kvg_send.at[to], kvg_all.at[seq], kvg_s.at[d], kvg_r.at[d], to)
        copy.start()
        kvg_copies.append(copy)

    qg_ref[...] = (dot(grad_score, k_diag, TN) * scale).astype(jnp.bfloat16)

    total = kvg_send[seq]
    for d, (_, source) in enumerate(ring):
        kvg_copies[d].wait_recv()
        total += kvg_all[source]
    kvg_ref[0] = total[:own].astype(jnp.bfloat16)
    kvg_ref[1] = total[own:].astype(jnp.bfloat16)

    sent = kv_copies + [pair_copy] + cross_copies + kvg_copies
    for copy in sent + list(far_copies.values()) + list(pass_copies.values()):
        copy.wait_send()


def store_kernel(qg_ref, kvg_ref, qg_hbm, kvg_hbm, sem):
    copies = [
        pltpu.make_async_copy(qg_ref, qg_hbm, sem.at[0]),
        pltpu.make_async_copy(kvg_ref, kvg_hbm, sem.at[1]),
    ]
    for copy in copies:
        copy.start()
    for copy in copies:
        copy.wait()


def body(queries, keys_values, out_grad, out_weight, enc_len, dec_len):
    seq_n, mp_n = lax.axis_size("seq"), lax.axis_size("mp")
    rows, width = queries.shape
    cols = out_grad.shape[1]
    cuts = len(pieces_of(cols))
    own = keys_values.shape[1]
    keys = own * seq_n
    kh = width // DH * keys
    far_n = max(mp_n // 2 - 1, 1)
    bf16, f32 = jnp.bfloat16, jnp.float32
    hbm = pl.BlockSpec(memory_space=pltpu.HBM)
    vmem = pl.BlockSpec(memory_space=pltpu.VMEM)
    dma = pltpu.SemaphoreType.DMA
    operands = [
        pltpu.with_memory_space_constraint(a, pltpu.HBM)
        for a in (enc_len, dec_len, queries, keys_values, out_grad, out_weight)
    ]
    results = pl.pallas_call(
        functools.partial(kernel, seq_n, mp_n),
        out_shape=(
            pltpu.VMEM((rows, width), bf16),
            pltpu.VMEM((2, own, width), bf16),
        ),
        in_specs=[hbm] * 6,
        out_specs=(vmem, vmem),
        scratch_shapes=[
            pltpu.SMEM((SEQS,), jnp.int32),
            pltpu.SMEM((SEQS,), jnp.int32),
            pltpu.VMEM((rows, width), bf16),
            pltpu.VMEM((mp_n, rows, cols), bf16),
            pltpu.VMEM((mp_n, width, cols), bf16),
            pltpu.VMEM((seq_n, 2, own, width), bf16),
            pltpu.VMEM((kh, width), f32),
            pltpu.VMEM((kh, width), f32),
            pltpu.VMEM((rows, width), f32),
            pltpu.VMEM((seq_n, 2 * own, width), f32),
            pltpu.VMEM((seq_n, 2 * own, width), f32),
            dma((2,)),
            dma,
            dma,
            dma((mp_n,)),
            dma,
            dma((seq_n,)),
            dma((seq_n,)),
            dma,
            dma,
            dma((far_n, cuts)),
            dma((far_n, cuts)),
            dma((far_n,)),
            dma((far_n,)),
            dma((far_n, cuts)),
            dma((far_n, cuts)),
            dma((seq_n,)),
            dma((seq_n,)),
        ],
        compiler_params=pltpu.CompilerParams(
            collective_id=0, has_side_effects=True, vmem_limit_bytes=48 * 2**20
        ),
        name="cross_attention_backward",
    )(*operands)
    results = [pltpu.with_memory_space_constraint(a, pltpu.VMEM) for a in results]
    return pl.pallas_call(
        store_kernel,
        out_shape=(
            jax.ShapeDtypeStruct((rows, width), bf16),
            jax.ShapeDtypeStruct((2, own, width), bf16),
        ),
        in_specs=[vmem, vmem],
        out_specs=(hbm, hbm),
        scratch_shapes=[dma((2,))],
        name="store_results",
    )(*results)


def solution(mesh):
    assert mesh.shape["sec"] == SEQS
    placed = (
        P(("sec", "seq"), "mp"),
        P(None, ("sec", "seq"), "mp"),
        P(("sec", "seq"), "mp"),
        P("mp", None),
        P(),
        P(),
    )
    return jax.shard_map(
        body,
        mesh=mesh,
        in_specs=placed,
        out_specs=(P(("sec", "seq"), "mp"), P(None, ("sec", "seq"), "mp")),
        check_vma=False,
    )
```

```python
import functools

import jax
import jax.numpy as jnp
from jax import lax
from jax.experimental import pallas as pl
from jax.experimental.pallas import tpu as pltpu
from jax.sharding import PartitionSpec as P

DH = 256
SEQS = 2
LANES = 128
MESH = pl.DeviceIdType.MESH
NN = (((1,), (0,)), ((), ()))
NT = (((1,), (1,)), ((), ()))
TN = (((0,), (0,)), ((), ()))


def dot(a, b, dims):
    return lax.dot_general(a, b, dims, preferred_element_type=jnp.float32)


def pieces_of(cols):
    edges = list(range(0, cols, max(cols // 4, LANES))) + [cols]
    middle = (edges[-2] + cols) // 2
    if middle % LANES == 0 and middle > edges[-2]:
        edges.insert(-1, middle)
    return list(zip(edges[:-1], edges[1:]))


def kernel(
    seq_n,
    mp_n,
    enc_hbm,
    dec_hbm,
    q_hbm,
    kv_hbm,
    x_hbm,
    w_hbm,
    qg_ref,
    kvg_ref,
    enc_buf,
    dec_buf,
    q_buf,
    x_all,
    w_buf,
    kv_all,
    k_rows,
    v_rows,
    vw_buf,
    kvg_send,
    kvg_all,
    len_sem,
    q_sem,
    x_sem,
    w_sem,
    kv_own_sem,
    kv_s,
    kv_r,
    pair_s,
    pair_r,
    far_s,
    far_r,
    cross_s,
    cross_r,
    pass_s,
    pass_r,
    kvg_s,
    kvg_r,
):
    sec = lax.axis_index("sec")
    seq = lax.axis_index("seq")
    mp = lax.axis_index("mp")
    rows, width = q_buf.shape
    cols = x_all.shape[2]
    pieces = pieces_of(cols)
    last = len(pieces) - 1
    own = kv_hbm.shape[1]
    heads = width // DH
    keys = own * seq_n
    kh = heads * keys

    chips = mp_n // 2
    chip, core = mp // 2, mp % 2
    pair = chip * 2 + 1 - core
    far = [
        (((chip + d) % chips) * 2 + core, ((chip + chips - d) % chips) * 2 + core)
        for d in range(1, chips)
    ]
    cross = [(to + 1 - 2 * core, source + 1 - 2 * core) for to, source in far]
    ring = [((seq + d) % seq_n, (seq + seq_n - d) % seq_n) for d in range(1, seq_n)]

    def to_mp(src, dst, send, recv, peer):
        return pltpu.make_async_remote_copy(
            src_ref=src,
            dst_ref=dst,
            send_sem=send,
            recv_sem=recv,
            device_id=(sec, seq, peer),
            device_id_type=MESH,
        )

    def to_seq(src, dst, send, recv, peer):
        return pltpu.make_async_remote_copy(
            src_ref=src,
            dst_ref=dst,
            send_sem=send,
            recv_sem=recv,
            device_id=(sec, peer, mp),
            device_id_type=MESH,
        )

    barrier = pltpu.get_barrier_semaphore()
    for to in [pair] + [to for to, _ in far + cross]:
        pl.semaphore_signal(barrier, inc=1, device_id=(sec, seq, to), device_id_type=MESH)
    for to, _ in ring:
        pl.semaphore_signal(barrier, inc=1, device_id=(sec, to, mp), device_id_type=MESH)

    x_load = pltpu.make_async_copy(x_hbm, x_all.at[mp], x_sem)
    x_load.start()
    pl.semaphore_wait(barrier, 1 + 2 * len(far) + len(ring))

    kv_copies = []
    for d, (to, _) in enumerate(ring):
        copy = to_seq(kv_hbm, kv_all.at[seq], kv_s.at[d], kv_r.at[d], to)
        copy.start()
        kv_copies.append(copy)
    x_load.wait()
    far_copies = {}
    for c, (start, end) in enumerate(pieces):
        at = (slice(None), pl.ds(start, end - start))
        for d, (to, _) in enumerate(far):
            slot = x_all.at[(mp,) + at]
            copy = to_mp(slot, slot, far_s.at[d, c], far_r.at[d, c], to)
            copy.start()
            far_copies[d, c] = copy
        if c == 0:
            pair_copy = to_mp(x_all.at[mp], x_all.at[mp], pair_s, pair_r, pair)
            pair_copy.start()
    cross_copies = []
    for d, (to, _) in enumerate(cross):
        slot = x_all.at[(mp,) + at]
        copy = to_mp(slot, slot, cross_s.at[d], cross_r.at[d], to)
        copy.start()
        cross_copies.append(copy)

    kv_load = pltpu.make_async_copy(kv_hbm, kv_all.at[seq], kv_own_sem)
    kv_load.start()
    q_load = pltpu.make_async_copy(q_hbm, q_buf, q_sem)
    q_load.start()
    enc_load = pltpu.make_async_copy(enc_hbm, enc_buf, len_sem.at[0])
    enc_load.start()
    dec_load = pltpu.make_async_copy(dec_hbm, dec_buf, len_sem.at[1])
    dec_load.start()
    order = [mp, pair] + [source for _, source in far + cross]
    w_loads = []
    for n, piece in enumerate(order):
        start = pl.multiple_of(piece * cols, cols)
        load = pltpu.make_async_copy(
            w_hbm.at[:, pl.ds(start, cols)], w_buf.at[piece], w_sem.at[n]
        )
        load.start()
        w_loads.append(load)

    kv_load.wait()
    for copy in kv_copies:
        copy.wait_recv()
    for t in range(seq_n):
        for h in range(heads):
            at = pl.ds(h * keys + t * own, own)
            k_rows[at, :] = kv_all[t, 0].astype(jnp.float32)
            v_rows[at, :] = kv_all[t, 1].astype(jnp.float32)
    row_head = lax.broadcasted_iota(jnp.int32, (kh, width), 0) // keys
    col_head = lax.broadcasted_iota(jnp.int32, (kh, width), 1) // DH
    diagonal = row_head == col_head
    k_diag = jnp.where(diagonal, k_rows[...], 0.0).astype(jnp.bfloat16)
    v_diag = jnp.where(diagonal, v_rows[...], 0.0).astype(jnp.bfloat16)

    scale = DH ** (-0.5)
    q_load.wait()
    scores = dot(k_diag, q_buf[...], NT) * scale
    key_at = lax.broadcasted_iota(jnp.int32, (keys, rows), 0)
    token_at = lax.broadcasted_iota(jnp.int32, (1, rows), 1) + seq * rows
    enc_load.wait()
    dec_load.wait()
    allowed = key_at < enc_buf[sec]
    valid = token_at < dec_buf[sec]
    probs = []
    for h in range(heads):
        s = jnp.where(allowed, scores[h * keys : (h + 1) * keys], -1e30)
        e = jnp.where(allowed, jnp.exp(s - jnp.max(s, axis=0, keepdims=True)), 0.0)
        e = e / jnp.sum(e, axis=0, keepdims=True)
        probs.append(jnp.where(valid, e, 0.0))
    prob = jnp.concatenate(probs, axis=0) if heads > 1 else probs[0]
    prob_bf16 = prob.astype(jnp.bfloat16)

    for load, source in zip(w_loads, order):
        load.wait()
        vw_buf[source] = dot(v_diag, w_buf[source], NN).astype(jnp.bfloat16)

    def parts_of(source, piece):
        at = slice(*piece)
        x = x_all[source, :, at]
        grad_prob = dot(vw_buf[source, :, at], x, NT)
        weighted = dot(prob_bf16, x, NN).astype(jnp.bfloat16)
        return grad_prob, dot(weighted, w_buf[source, :, at], NT)

    grad_prob, value_part = parts_of(mp, (0, cols))

    def add(source, piece):
        more_prob, more_value = parts_of(source, piece)
        return grad_prob + more_prob, value_part + more_value

    pair_copy.wait_recv()
    grad_prob, value_part = add(pair, (0, cols))

    pass_copies = {}
    for c, piece in enumerate(pieces):
        for d, (_, source) in enumerate(far):
            far_copies[d, c].wait_recv()
            if c < last:
                slot = x_all.at[source, :, pl.ds(piece[0], piece[1] - piece[0])]
                copy = to_mp(slot, slot, pass_s.at[d, c], pass_r.at[d, c], pair)
                copy.start()
                pass_copies[d, c] = copy
        for _, source in far:
            grad_prob, value_part = add(source, piece)
        if c > 0:
            for d, (_, source) in enumerate(cross):
                pass_copies[d, c - 1].wait_recv()
                grad_prob, value_part = add(source, pieces[c - 1])
    for d, (_, source) in enumerate(cross):
        cross_copies[d].wait_recv()
        grad_prob, value_part = add(source, pieces[last])

    grads = []
    for h in range(heads):
        at = slice(h * keys, (h + 1) * keys)
        delta = jnp.sum(prob[at] * grad_prob[at], axis=0, keepdims=True)
        grads.append(prob[at] * (grad_prob[at] - delta))
    grad_score = (jnp.concatenate(grads, axis=0) if heads > 1 else grads[0]).astype(jnp.bfloat16)
    key_part = dot(grad_score, q_buf[...], NN) * scale

    def own_head(part):
        part = jnp.where(diagonal, part, 0.0)
        return sum(part[h * keys : (h + 1) * keys] for h in range(heads))

    key_part, value_part = own_head(key_part), own_head(value_part)
    for t in range(seq_n):
        kvg_send[t, pl.ds(0, own), :] = key_part[t * own : (t + 1) * own]
        kvg_send[t, pl.ds(own, own), :] = value_part[t * own : (t + 1) * own]
    kvg_copies = []
    for d, (to, _) in enumerate(ring):
        copy = to_seq(kvg_send.at[to], kvg_all.at[seq], kvg_s.at[d], kvg_r.at[d], to)
        copy.start()
        kvg_copies.append(copy)

    qg_ref[...] = (dot(grad_score, k_diag, TN) * scale).astype(jnp.bfloat16)

    total = kvg_send[seq]
    for d, (_, source) in enumerate(ring):
        kvg_copies[d].wait_recv()
        total += kvg_all[source]
    kvg_ref[0] = total[:own].astype(jnp.bfloat16)
    kvg_ref[1] = total[own:].astype(jnp.bfloat16)

    sent = kv_copies + [pair_copy] + cross_copies + kvg_copies
    for copy in sent + list(far_copies.values()) + list(pass_copies.values()):
        copy.wait_send()


def store_kernel(qg_ref, kvg_ref, qg_hbm, kvg_hbm, sem):
    copies = [
        pltpu.make_async_copy(qg_ref, qg_hbm, sem.at[0]),
        pltpu.make_async_copy(kvg_ref, kvg_hbm, sem.at[1]),
    ]
    for copy in copies:
        copy.start()
    for copy in copies:
        copy.wait()


def body(queries, keys_values, out_grad, out_weight, enc_len, dec_len):
    seq_n, mp_n = lax.axis_size("seq"), lax.axis_size("mp")
    rows, width = queries.shape
    cols = out_grad.shape[1]
    cuts = len(pieces_of(cols))
    own = keys_values.shape[1]
    keys = own * seq_n
    kh = width // DH * keys
    far_n = max(mp_n // 2 - 1, 1)
    bf16, f32 = jnp.bfloat16, jnp.float32
    hbm = pl.BlockSpec(memory_space=pltpu.HBM)
    vmem = pl.BlockSpec(memory_space=pltpu.VMEM)
    dma = pltpu.SemaphoreType.DMA
    operands = [
        pltpu.with_memory_space_constraint(a, pltpu.HBM)
        for a in (enc_len, dec_len, queries, keys_values, out_grad, out_weight)
    ]
    results = pl.pallas_call(
        functools.partial(kernel, seq_n, mp_n),
        out_shape=(
            pltpu.VMEM((rows, width), bf16),
            pltpu.VMEM((2, own, width), bf16),
        ),
        in_specs=[hbm] * 6,
        out_specs=(vmem, vmem),
        scratch_shapes=[
            pltpu.SMEM((SEQS,), jnp.int32),
            pltpu.SMEM((SEQS,), jnp.int32),
            pltpu.VMEM((rows, width), bf16),
            pltpu.VMEM((mp_n, rows, cols), bf16),
            pltpu.VMEM((mp_n, width, cols), bf16),
            pltpu.VMEM((seq_n, 2, own, width), bf16),
            pltpu.VMEM((kh, width), f32),
            pltpu.VMEM((kh, width), f32),
            pltpu.VMEM((mp_n, kh, cols), bf16),
            pltpu.VMEM((seq_n, 2 * own, width), f32),
            pltpu.VMEM((seq_n, 2 * own, width), f32),
            dma((2,)),
            dma,
            dma,
            dma((mp_n,)),
            dma,
            dma((seq_n,)),
            dma((seq_n,)),
            dma,
            dma,
            dma((far_n, cuts)),
            dma((far_n, cuts)),
            dma((far_n,)),
            dma((far_n,)),
            dma((far_n, cuts)),
            dma((far_n, cuts)),
            dma((seq_n,)),
            dma((seq_n,)),
        ],
        compiler_params=pltpu.CompilerParams(
            collective_id=0, has_side_effects=True, vmem_limit_bytes=48 * 2**20
        ),
        name="cross_attention_backward",
    )(*operands)
    results = [pltpu.with_memory_space_constraint(a, pltpu.VMEM) for a in results]
    return pl.pallas_call(
        store_kernel,
        out_shape=(
            jax.ShapeDtypeStruct((rows, width), bf16),
            jax.ShapeDtypeStruct((2, own, width), bf16),
        ),
        in_specs=[vmem, vmem],
        out_specs=(hbm, hbm),
        scratch_shapes=[dma((2,))],
        name="store_results",
    )(*results)


def solution(mesh):
    assert mesh.shape["sec"] == SEQS
    placed = (
        P(("sec", "seq"), "mp"),
        P(None, ("sec", "seq"), "mp"),
        P(("sec", "seq"), "mp"),
        P("mp", None),
        P(),
        P(),
    )
    return jax.shard_map(
        body,
        mesh=mesh,
        in_specs=placed,
        out_specs=(P(("sec", "seq"), "mp"), P(None, ("sec", "seq"), "mp")),
        check_vma=False,
    )
```

```python
import functools

import jax
import jax.numpy as jnp
from jax import lax
from jax.experimental import pallas as pl
from jax.experimental.pallas import tpu as pltpu
from jax.sharding import PartitionSpec as P

DH = 256
SEQS = 2
LANES = 128
MESH = pl.DeviceIdType.MESH
NN = (((1,), (0,)), ((), ()))
NT = (((1,), (1,)), ((), ()))
TN = (((0,), (0,)), ((), ()))


def dot(a, b, dims):
    return lax.dot_general(a, b, dims, preferred_element_type=jnp.float32)


def pieces_of(cols):
    edges = list(range(0, cols, max(cols // 4, LANES))) + [cols]
    middle = (edges[-2] + cols) // 2
    if middle % LANES == 0 and middle > edges[-2]:
        edges.insert(-1, middle)
    return list(zip(edges[:-1], edges[1:]))


def kernel(
    seq_n,
    mp_n,
    enc_hbm,
    dec_hbm,
    q_hbm,
    kv_hbm,
    x_hbm,
    w_hbm,
    qg_ref,
    kvg_ref,
    enc_buf,
    dec_buf,
    q_buf,
    x_all,
    w_buf,
    kv_all,
    k_rows,
    v_rows,
    vw_buf,
    kvg_send,
    kvg_all,
    len_sem,
    q_sem,
    x_sem,
    w_sem,
    kv_own_sem,
    kv_s,
    kv_r,
    pair_s,
    pair_r,
    far_s,
    far_r,
    cross_s,
    cross_r,
    pass_s,
    pass_r,
    kvg_s,
    kvg_r,
):
    sec = lax.axis_index("sec")
    seq = lax.axis_index("seq")
    mp = lax.axis_index("mp")
    rows, width = q_buf.shape
    cols = x_all.shape[2]
    pieces = pieces_of(cols)
    last = len(pieces) - 1
    own = kv_hbm.shape[1]
    heads = width // DH
    keys = own * seq_n
    kh = heads * keys

    chips = mp_n // 2
    chip, core = mp // 2, mp % 2
    pair = chip * 2 + 1 - core
    far = [
        (((chip + d) % chips) * 2 + core, ((chip + chips - d) % chips) * 2 + core)
        for d in range(1, chips)
    ]
    cross = [(to + 1 - 2 * core, source + 1 - 2 * core) for to, source in far]
    ring = [((seq + d) % seq_n, (seq + seq_n - d) % seq_n) for d in range(1, seq_n)]

    def to_mp(src, dst, send, recv, peer):
        return pltpu.make_async_remote_copy(
            src_ref=src,
            dst_ref=dst,
            send_sem=send,
            recv_sem=recv,
            device_id=(sec, seq, peer),
            device_id_type=MESH,
        )

    def to_seq(src, dst, send, recv, peer):
        return pltpu.make_async_remote_copy(
            src_ref=src,
            dst_ref=dst,
            send_sem=send,
            recv_sem=recv,
            device_id=(sec, peer, mp),
            device_id_type=MESH,
        )

    barrier = pltpu.get_barrier_semaphore()
    for to in [pair] + [to for to, _ in far + cross]:
        pl.semaphore_signal(barrier, inc=1, device_id=(sec, seq, to), device_id_type=MESH)
    for to, _ in ring:
        pl.semaphore_signal(barrier, inc=1, device_id=(sec, to, mp), device_id_type=MESH)

    x_load = pltpu.make_async_copy(x_hbm, x_all.at[mp], x_sem)
    x_load.start()
    pl.semaphore_wait(barrier, 1 + 2 * len(far) + len(ring))

    half = rows // 2
    cuts = [(pl.ds(0, rows), pl.ds(a, b - a)) for a, b in pieces[:-1]]
    tail = pl.ds(pieces[-1][0], pieces[-1][1] - pieces[-1][0])
    cuts += [(pl.ds(0, half), tail), (pl.ds(half, rows - half), tail)]
    x_load.wait()
    far_copies = {}
    for c, at in enumerate(cuts):
        slot = x_all.at[(mp,) + at]
        for d, (to, _) in enumerate(far):
            copy = to_mp(slot, slot, far_s.at[d, c], far_r.at[d, c], to)
            copy.start()
            far_copies[d, c] = copy
        if c == 0:
            pair_copy = to_mp(x_all.at[mp], x_all.at[mp], pair_s, pair_r, pair)
            pair_copy.start()
    cross_copies = []
    for d, (to, _) in enumerate(cross):
        slot = x_all.at[(mp,) + cuts[-1]]
        copy = to_mp(slot, slot, cross_s.at[d], cross_r.at[d], to)
        copy.start()
        cross_copies.append(copy)

    kv_copies = []
    for d, (to, _) in enumerate(ring):
        copy = to_seq(kv_hbm, kv_all.at[seq], kv_s.at[d], kv_r.at[d], to)
        copy.start()
        kv_copies.append(copy)

    kv_load = pltpu.make_async_copy(kv_hbm, kv_all.at[seq], kv_own_sem)
    kv_load.start()
    q_load = pltpu.make_async_copy(q_hbm, q_buf, q_sem)
    q_load.start()
    enc_load = pltpu.make_async_copy(enc_hbm, enc_buf, len_sem.at[0])
    enc_load.start()
    dec_load = pltpu.make_async_copy(dec_hbm, dec_buf, len_sem.at[1])
    dec_load.start()
    order = [mp, pair] + [source for _, source in far + cross]
    w_loads = []
    for n, piece in enumerate(order):
        start = pl.multiple_of(piece * cols, cols)
        load = pltpu.make_async_copy(
            w_hbm.at[:, pl.ds(start, cols)], w_buf.at[piece], w_sem.at[n]
        )
        load.start()
        w_loads.append(load)

    kv_load.wait()
    for copy in kv_copies:
        copy.wait_recv()
    for t in range(seq_n):
        for h in range(heads):
            at = pl.ds(h * keys + t * own, own)
            k_rows[at, :] = kv_all[t, 0].astype(jnp.float32)
            v_rows[at, :] = kv_all[t, 1].astype(jnp.float32)
    row_head = lax.broadcasted_iota(jnp.int32, (kh, width), 0) // keys
    col_head = lax.broadcasted_iota(jnp.int32, (kh, width), 1) // DH
    diagonal = row_head == col_head
    k_diag = jnp.where(diagonal, k_rows[...], 0.0).astype(jnp.bfloat16)
    v_diag = jnp.where(diagonal, v_rows[...], 0.0).astype(jnp.bfloat16)

    scale = DH ** (-0.5)
    q_load.wait()
    scores = dot(k_diag, q_buf[...], NT) * scale
    key_at = lax.broadcasted_iota(jnp.int32, (keys, rows), 0)
    token_at = lax.broadcasted_iota(jnp.int32, (1, rows), 1) + seq * rows
    enc_load.wait()
    dec_load.wait()
    allowed = key_at < enc_buf[sec]
    valid = token_at < dec_buf[sec]
    probs = []
    for h in range(heads):
        s = jnp.where(allowed, scores[h * keys : (h + 1) * keys], -1e30)
        e = jnp.where(allowed, jnp.exp(s - jnp.max(s, axis=0, keepdims=True)), 0.0)
        e = e / jnp.sum(e, axis=0, keepdims=True)
        probs.append(jnp.where(valid, e, 0.0))
    prob = jnp.concatenate(probs, axis=0) if heads > 1 else probs[0]
    prob_bf16 = prob.astype(jnp.bfloat16)

    for load, source in zip(w_loads, order):
        load.wait()
        vw_buf[source] = dot(v_diag, w_buf[source], NN).astype(jnp.bfloat16)

    def parts_of(source, piece):
        at = slice(*piece)
        x = x_all[source, :, at]
        grad_prob = dot(vw_buf[source, :, at], x, NT)
        weighted = dot(prob_bf16, x, NN).astype(jnp.bfloat16)
        return grad_prob, dot(weighted, w_buf[source, :, at], NT)

    grad_prob, value_part = parts_of(mp, (0, cols))

    def add(source, piece):
        more_prob, more_value = parts_of(source, piece)
        return grad_prob + more_prob, value_part + more_value

    pair_copy.wait_recv()
    grad_prob, value_part = add(pair, (0, cols))

    pass_copies = {}
    for c, at in enumerate(cuts[:-1]):
        for d, (_, source) in enumerate(far):
            far_copies[d, c].wait_recv()
            slot = x_all.at[(source,) + at]
            copy = to_mp(slot, slot, pass_s.at[d, c], pass_r.at[d, c], pair)
            copy.start()
            pass_copies[d, c] = copy
        if c < last:
            for _, source in far:
                grad_prob, value_part = add(source, pieces[c])
        if c > 0:
            for d, (_, source) in enumerate(cross):
                pass_copies[d, c - 1].wait_recv()
                grad_prob, value_part = add(source, pieces[c - 1])
    for d, (_, source) in enumerate(far):
        far_copies[d, last + 1].wait_recv()
        grad_prob, value_part = add(source, pieces[last])
    for d, (_, source) in enumerate(cross):
        pass_copies[d, last].wait_recv()
        cross_copies[d].wait_recv()
        grad_prob, value_part = add(source, pieces[last])

    grads = []
    for h in range(heads):
        at = slice(h * keys, (h + 1) * keys)
        delta = jnp.sum(prob[at] * grad_prob[at], axis=0, keepdims=True)
        grads.append(prob[at] * (grad_prob[at] - delta))
    grad_score = (jnp.concatenate(grads, axis=0) if heads > 1 else grads[0]).astype(jnp.bfloat16)
    key_part = dot(grad_score, q_buf[...], NN) * scale

    def own_head(part):
        part = jnp.where(diagonal, part, 0.0)
        return sum(part[h * keys : (h + 1) * keys] for h in range(heads))

    key_part, value_part = own_head(key_part), own_head(value_part)
    for t in range(seq_n):
        at = slice(t * own, (t + 1) * own)
        kvg_send[t, 0] = key_part[at].astype(jnp.bfloat16)
        kvg_send[t, 1] = value_part[at].astype(jnp.bfloat16)
    kvg_copies = []
    for d, (to, _) in enumerate(ring):
        copy = to_seq(kvg_send.at[to], kvg_all.at[seq], kvg_s.at[d], kvg_r.at[d], to)
        copy.start()
        kvg_copies.append(copy)

    qg_ref[...] = (dot(grad_score, k_diag, TN) * scale).astype(jnp.bfloat16)

    sent = kv_copies + [pair_copy] + cross_copies
    for copy in sent + list(far_copies.values()) + list(pass_copies.values()):
        copy.wait_send()

    sums = [kvg_send[seq, n].astype(jnp.float32) for n in range(2)]
    for d, (_, source) in enumerate(ring):
        kvg_copies[d].wait_recv()
        sums = [sums[n] + kvg_all[source, n].astype(jnp.float32) for n in range(2)]
    for n in range(2):
        kvg_ref[n] = sums[n].astype(jnp.bfloat16)
    for copy in kvg_copies:
        copy.wait_send()


def store_kernel(qg_ref, kvg_ref, qg_hbm, kvg_hbm, sem):
    copies = [
        pltpu.make_async_copy(qg_ref, qg_hbm, sem.at[0]),
        pltpu.make_async_copy(kvg_ref, kvg_hbm, sem.at[1]),
    ]
    for copy in copies:
        copy.start()
    for copy in copies:
        copy.wait()


def body(queries, keys_values, out_grad, out_weight, enc_len, dec_len):
    seq_n, mp_n = lax.axis_size("seq"), lax.axis_size("mp")
    rows, width = queries.shape
    cols = out_grad.shape[1]
    cuts = len(pieces_of(cols)) + 1
    own = keys_values.shape[1]
    keys = own * seq_n
    kh = width // DH * keys
    far_n = max(mp_n // 2 - 1, 1)
    bf16, f32 = jnp.bfloat16, jnp.float32
    hbm = pl.BlockSpec(memory_space=pltpu.HBM)
    vmem = pl.BlockSpec(memory_space=pltpu.VMEM)
    dma = pltpu.SemaphoreType.DMA
    operands = [
        pltpu.with_memory_space_constraint(a, pltpu.HBM)
        for a in (enc_len, dec_len, queries, keys_values, out_grad, out_weight)
    ]
    results = pl.pallas_call(
        functools.partial(kernel, seq_n, mp_n),
        out_shape=(
            pltpu.VMEM((rows, width), bf16),
            pltpu.VMEM((2, own, width), bf16),
        ),
        in_specs=[hbm] * 6,
        out_specs=(vmem, vmem),
        scratch_shapes=[
            pltpu.SMEM((SEQS,), jnp.int32),
            pltpu.SMEM((SEQS,), jnp.int32),
            pltpu.VMEM((rows, width), bf16),
            pltpu.VMEM((mp_n, rows, cols), bf16),
            pltpu.VMEM((mp_n, width, cols), bf16),
            pltpu.VMEM((seq_n, 2, own, width), bf16),
            pltpu.VMEM((kh, width), f32),
            pltpu.VMEM((kh, width), f32),
            pltpu.VMEM((mp_n, kh, cols), bf16),
            pltpu.VMEM((seq_n, 2, own, width), bf16),
            pltpu.VMEM((seq_n, 2, own, width), bf16),
            dma((2,)),
            dma,
            dma,
            dma((mp_n,)),
            dma,
            dma((seq_n,)),
            dma((seq_n,)),
            dma,
            dma,
            dma((far_n, cuts)),
            dma((far_n, cuts)),
            dma((far_n,)),
            dma((far_n,)),
            dma((far_n, cuts)),
            dma((far_n, cuts)),
            dma((seq_n,)),
            dma((seq_n,)),
        ],
        compiler_params=pltpu.CompilerParams(
            collective_id=0, has_side_effects=True, vmem_limit_bytes=48 * 2**20
        ),
        name="cross_attention_backward",
    )(*operands)
    results = [pltpu.with_memory_space_constraint(a, pltpu.VMEM) for a in results]
    return pl.pallas_call(
        store_kernel,
        out_shape=(
            jax.ShapeDtypeStruct((rows, width), bf16),
            jax.ShapeDtypeStruct((2, own, width), bf16),
        ),
        in_specs=[vmem, vmem],
        out_specs=(hbm, hbm),
        scratch_shapes=[dma((2,))],
        name="store_results",
    )(*results)


def solution(mesh):
    assert mesh.shape["sec"] == SEQS
    placed = (
        P(("sec", "seq"), "mp"),
        P(None, ("sec", "seq"), "mp"),
        P(("sec", "seq"), "mp"),
        P("mp", None),
        P(),
        P(),
    )
    return jax.shard_map(
        body,
        mesh=mesh,
        in_specs=placed,
        out_specs=(P(("sec", "seq"), "mp"), P(None, ("sec", "seq"), "mp")),
        check_vma=False,
    )
```

```python
import functools

import jax
import jax.numpy as jnp
from jax import lax
from jax.experimental import pallas as pl
from jax.experimental.pallas import tpu as pltpu
from jax.sharding import PartitionSpec as P

DH = 256
SEQS = 2
LANES = 128
MESH = pl.DeviceIdType.MESH
NN = (((1,), (0,)), ((), ()))
NT = (((1,), (1,)), ((), ()))
TN = (((0,), (0,)), ((), ()))


def dot(a, b, dims):
    return lax.dot_general(a, b, dims, preferred_element_type=jnp.float32)


def pieces_of(cols):
    edges = list(range(0, cols, max(cols // 4, LANES))) + [cols]
    middle = (edges[-2] + cols) // 2
    if middle % LANES == 0 and middle > edges[-2]:
        edges.insert(-1, middle)
    return list(zip(edges[:-1], edges[1:]))


def kernel(
    seq_n,
    mp_n,
    enc_hbm,
    dec_hbm,
    q_hbm,
    kv_hbm,
    x_hbm,
    w_hbm,
    qg_ref,
    kvg_ref,
    enc_buf,
    dec_buf,
    q_buf,
    x_all,
    w_buf,
    kv_all,
    k_rows,
    v_rows,
    vw_buf,
    kvg_send,
    kvg_all,
    len_sem,
    q_sem,
    x_sem,
    w_sem,
    kv_own_sem,
    kv_s,
    kv_r,
    pair_s,
    pair_r,
    far_s,
    far_r,
    cross_s,
    cross_r,
    pass_s,
    pass_r,
    kvg_s,
    kvg_r,
):
    sec = lax.axis_index("sec")
    seq = lax.axis_index("seq")
    mp = lax.axis_index("mp")
    rows, width = q_buf.shape
    cols = x_all.shape[2]
    pieces = pieces_of(cols)
    last = len(pieces) - 1
    own = kv_hbm.shape[1]
    heads = width // DH
    keys = own * seq_n
    kh = heads * keys

    chips = mp_n // 2
    chip, core = mp // 2, mp % 2
    pair = chip * 2 + 1 - core
    far = [
        (((chip + d) % chips) * 2 + core, ((chip + chips - d) % chips) * 2 + core)
        for d in range(1, chips)
    ]
    cross = [(to + 1 - 2 * core, source + 1 - 2 * core) for to, source in far]
    ring = [((seq + d) % seq_n, (seq + seq_n - d) % seq_n) for d in range(1, seq_n)]

    def to_mp(src, dst, send, recv, peer):
        return pltpu.make_async_remote_copy(
            src_ref=src,
            dst_ref=dst,
            send_sem=send,
            recv_sem=recv,
            device_id=(sec, seq, peer),
            device_id_type=MESH,
        )

    def to_seq(src, dst, send, recv, peer):
        return pltpu.make_async_remote_copy(
            src_ref=src,
            dst_ref=dst,
            send_sem=send,
            recv_sem=recv,
            device_id=(sec, peer, mp),
            device_id_type=MESH,
        )

    barrier = pltpu.get_barrier_semaphore()
    for to in [pair] + [to for to, _ in far + cross]:
        pl.semaphore_signal(barrier, inc=1, device_id=(sec, seq, to), device_id_type=MESH)
    for to, _ in ring:
        pl.semaphore_signal(barrier, inc=1, device_id=(sec, to, mp), device_id_type=MESH)

    x_load = pltpu.make_async_copy(x_hbm, x_all.at[mp], x_sem)
    x_load.start()
    kv_load = pltpu.make_async_copy(kv_hbm, kv_all.at[seq], kv_own_sem)
    kv_load.start()
    q_load = pltpu.make_async_copy(q_hbm, q_buf, q_sem)
    q_load.start()
    enc_load = pltpu.make_async_copy(enc_hbm, enc_buf, len_sem.at[0])
    enc_load.start()
    dec_load = pltpu.make_async_copy(dec_hbm, dec_buf, len_sem.at[1])
    dec_load.start()
    order = [mp, pair] + [source for _, source in far + cross]
    w_loads = []
    for n, piece in enumerate(order):
        start = pl.multiple_of(piece * cols, cols)
        load = pltpu.make_async_copy(
            w_hbm.at[:, pl.ds(start, cols)], w_buf.at[piece], w_sem.at[n]
        )
        load.start(priority=1)
        w_loads.append(load)

    pl.semaphore_wait(barrier, 1 + 2 * len(far) + len(ring))

    kv_copies = []
    for d, (to, _) in enumerate(ring):
        copy = to_seq(kv_hbm, kv_all.at[seq], kv_s.at[d], kv_r.at[d], to)
        copy.start()
        kv_copies.append(copy)
    x_load.wait()
    far_copies = {}
    for c, (start, end) in enumerate(pieces):
        at = (slice(None), pl.ds(start, end - start))
        for d, (to, _) in enumerate(far):
            slot = x_all.at[(mp,) + at]
            copy = to_mp(slot, slot, far_s.at[d, c], far_r.at[d, c], to)
            copy.start()
            far_copies[d, c] = copy
        if c == 0:
            pair_copy = to_mp(x_all.at[mp], x_all.at[mp], pair_s, pair_r, pair)
            pair_copy.start()
    cross_copies = []
    for d, (to, _) in enumerate(cross):
        slot = x_all.at[(mp,) + at]
        copy = to_mp(slot, slot, cross_s.at[d], cross_r.at[d], to)
        copy.start()
        cross_copies.append(copy)

    kv_load.wait()
    for copy in kv_copies:
        copy.wait_recv()
    for t in range(seq_n):
        for h in range(heads):
            at = pl.ds(h * keys + t * own, own)
            k_rows[at, :] = kv_all[t, 0].astype(jnp.float32)
            v_rows[at, :] = kv_all[t, 1].astype(jnp.float32)
    row_head = lax.broadcasted_iota(jnp.int32, (kh, width), 0) // keys
    col_head = lax.broadcasted_iota(jnp.int32, (kh, width), 1) // DH
    diagonal = row_head == col_head
    k_diag = jnp.where(diagonal, k_rows[...], 0.0).astype(jnp.bfloat16)
    v_diag = jnp.where(diagonal, v_rows[...], 0.0).astype(jnp.bfloat16)

    scale = DH ** (-0.5)
    q_load.wait()
    scores = dot(k_diag, q_buf[...], NT) * scale
    key_at = lax.broadcasted_iota(jnp.int32, (keys, rows), 0)
    token_at = lax.broadcasted_iota(jnp.int32, (1, rows), 1) + seq * rows
    enc_load.wait()
    dec_load.wait()
    allowed = key_at < enc_buf[sec]
    valid = token_at < dec_buf[sec]
    probs = []
    for h in range(heads):
        s = jnp.where(allowed, scores[h * keys : (h + 1) * keys], -1e30)
        e = jnp.where(allowed, jnp.exp(s - jnp.max(s, axis=0, keepdims=True)), 0.0)
        e = e / jnp.sum(e, axis=0, keepdims=True)
        probs.append(jnp.where(valid, e, 0.0))
    prob = jnp.concatenate(probs, axis=0) if heads > 1 else probs[0]
    prob_bf16 = prob.astype(jnp.bfloat16)

    for load, source in zip(w_loads, order):
        load.wait()
        vw_buf[source] = dot(v_diag, w_buf[source], NN).astype(jnp.bfloat16)

    def parts_of(source, piece):
        at = slice(*piece)
        x = x_all[source, :, at]
        grad_prob = dot(vw_buf[source, :, at], x, NT)
        weighted = dot(prob_bf16, x, NN).astype(jnp.bfloat16)
        return grad_prob, dot(weighted, w_buf[source, :, at], NT)

    grad_prob, value_part = parts_of(mp, (0, cols))

    def add(source, piece):
        more_prob, more_value = parts_of(source, piece)
        return grad_prob + more_prob, value_part + more_value

    pair_copy.wait_recv()
    grad_prob, value_part = add(pair, (0, cols))

    pass_copies = {}
    for c, piece in enumerate(pieces):
        for d, (_, source) in enumerate(far):
            far_copies[d, c].wait_recv()
            if c < last:
                slot = x_all.at[source, :, pl.ds(piece[0], piece[1] - piece[0])]
                copy = to_mp(slot, slot, pass_s.at[d, c], pass_r.at[d, c], pair)
                copy.start()
                pass_copies[d, c] = copy
        for _, source in far:
            grad_prob, value_part = add(source, piece)
        if c > 0:
            for d, (_, source) in enumerate(cross):
                pass_copies[d, c - 1].wait_recv()
                grad_prob, value_part = add(source, pieces[c - 1])
    for d, (_, source) in enumerate(cross):
        cross_copies[d].wait_recv()
        grad_prob, value_part = add(source, pieces[last])

    grads = []
    for h in range(heads):
        at = slice(h * keys, (h + 1) * keys)
        delta = jnp.sum(prob[at] * grad_prob[at], axis=0, keepdims=True)
        grads.append(prob[at] * (grad_prob[at] - delta))
    grad_score = (jnp.concatenate(grads, axis=0) if heads > 1 else grads[0]).astype(jnp.bfloat16)
    key_part = dot(grad_score, q_buf[...], NN) * scale

    def own_head(part):
        part = jnp.where(diagonal, part, 0.0)
        return sum(part[h * keys : (h + 1) * keys] for h in range(heads))

    key_part, value_part = own_head(key_part), own_head(value_part)
    for t in range(seq_n):
        kvg_send[t, pl.ds(0, own), :] = key_part[t * own : (t + 1) * own]
        kvg_send[t, pl.ds(own, own), :] = value_part[t * own : (t + 1) * own]
    kvg_copies = []
    for d, (to, _) in enumerate(ring):
        copy = to_seq(kvg_send.at[to], kvg_all.at[seq], kvg_s.at[d], kvg_r.at[d], to)
        copy.start()
        kvg_copies.append(copy)

    qg_ref[...] = (dot(grad_score, k_diag, TN) * scale).astype(jnp.bfloat16)

    sent = kv_copies + [pair_copy] + cross_copies
    for copy in sent + list(far_copies.values()) + list(pass_copies.values()):
        copy.wait_send()

    total = kvg_send[seq]
    for d, (_, source) in enumerate(ring):
        kvg_copies[d].wait_recv()
        total += kvg_all[source]
    kvg_ref[0] = total[:own].astype(jnp.bfloat16)
    kvg_ref[1] = total[own:].astype(jnp.bfloat16)

    for copy in kvg_copies:
        copy.wait_send()


def store_kernel(qg_ref, kvg_ref, qg_hbm, kvg_hbm, sem):
    copies = [
        pltpu.make_async_copy(qg_ref, qg_hbm, sem.at[0]),
        pltpu.make_async_copy(kvg_ref, kvg_hbm, sem.at[1]),
    ]
    for copy in copies:
        copy.start()
    for copy in copies:
        copy.wait()


def body(queries, keys_values, out_grad, out_weight, enc_len, dec_len):
    seq_n, mp_n = lax.axis_size("seq"), lax.axis_size("mp")
    rows, width = queries.shape
    cols = out_grad.shape[1]
    cuts = len(pieces_of(cols))
    own = keys_values.shape[1]
    keys = own * seq_n
    kh = width // DH * keys
    far_n = max(mp_n // 2 - 1, 1)
    bf16, f32 = jnp.bfloat16, jnp.float32
    hbm = pl.BlockSpec(memory_space=pltpu.HBM)
    vmem = pl.BlockSpec(memory_space=pltpu.VMEM)
    dma = pltpu.SemaphoreType.DMA
    operands = [
        pltpu.with_memory_space_constraint(a, pltpu.HBM)
        for a in (enc_len, dec_len, queries, keys_values, out_grad, out_weight)
    ]
    results = pl.pallas_call(
        functools.partial(kernel, seq_n, mp_n),
        out_shape=(
            pltpu.VMEM((rows, width), bf16),
            pltpu.VMEM((2, own, width), bf16),
        ),
        in_specs=[hbm] * 6,
        out_specs=(vmem, vmem),
        scratch_shapes=[
            pltpu.SMEM((SEQS,), jnp.int32),
            pltpu.SMEM((SEQS,), jnp.int32),
            pltpu.VMEM((rows, width), bf16),
            pltpu.VMEM((mp_n, rows, cols), bf16),
            pltpu.VMEM((mp_n, width, cols), bf16),
            pltpu.VMEM((seq_n, 2, own, width), bf16),
            pltpu.VMEM((kh, width), f32),
            pltpu.VMEM((kh, width), f32),
            pltpu.VMEM((mp_n, kh, cols), bf16),
            pltpu.VMEM((seq_n, 2 * own, width), f32),
            pltpu.VMEM((seq_n, 2 * own, width), f32),
            dma((2,)),
            dma,
            dma,
            dma((mp_n,)),
            dma,
            dma((seq_n,)),
            dma((seq_n,)),
            dma,
            dma,
            dma((far_n, cuts)),
            dma((far_n, cuts)),
            dma((far_n,)),
            dma((far_n,)),
            dma((far_n, cuts)),
            dma((far_n, cuts)),
            dma((seq_n,)),
            dma((seq_n,)),
        ],
        compiler_params=pltpu.CompilerParams(
            collective_id=0, has_side_effects=True, vmem_limit_bytes=48 * 2**20
        ),
        name="cross_attention_backward",
    )(*operands)
    results = [pltpu.with_memory_space_constraint(a, pltpu.VMEM) for a in results]
    return pl.pallas_call(
        store_kernel,
        out_shape=(
            jax.ShapeDtypeStruct((rows, width), bf16),
            jax.ShapeDtypeStruct((2, own, width), bf16),
        ),
        in_specs=[vmem, vmem],
        out_specs=(hbm, hbm),
        scratch_shapes=[dma((2,))],
        name="store_results",
    )(*results)


def solution(mesh):
    assert mesh.shape["sec"] == SEQS
    placed = (
        P(("sec", "seq"), "mp"),
        P(None, ("sec", "seq"), "mp"),
        P(("sec", "seq"), "mp"),
        P("mp", None),
        P(),
        P(),
    )
    return jax.shard_map(
        body,
        mesh=mesh,
        in_specs=placed,
        out_specs=(P(("sec", "seq"), "mp"), P(None, ("sec", "seq"), "mp")),
        check_vma=False,
    )
```

```python
import functools

import jax
import jax.numpy as jnp
from jax import lax
from jax.experimental import pallas as pl
from jax.experimental.pallas import tpu as pltpu
from jax.sharding import PartitionSpec as P

DH = 256
SEQS = 2
LANES = 128
MESH = pl.DeviceIdType.MESH
NN = (((1,), (0,)), ((), ()))
NT = (((1,), (1,)), ((), ()))
TN = (((0,), (0,)), ((), ()))


def dot(a, b, dims):
    return lax.dot_general(a, b, dims, preferred_element_type=jnp.float32)


def pieces_of(cols):
    edges = list(range(0, cols, max(cols // 4, LANES))) + [cols]
    middle = (edges[-2] + cols) // 2
    if middle % LANES == 0 and middle > edges[-2]:
        edges.insert(-1, middle)
    return list(zip(edges[:-1], edges[1:]))


def kernel(
    seq_n,
    mp_n,
    enc_hbm,
    dec_hbm,
    q_hbm,
    kv_hbm,
    x_hbm,
    w_hbm,
    qg_ref,
    kvg_ref,
    enc_buf,
    dec_buf,
    q_buf,
    x_all,
    w_buf,
    kv_all,
    k_rows,
    v_rows,
    vw_buf,
    kvg_send,
    kvg_all,
    len_sem,
    q_sem,
    x_sem,
    w_sem,
    kv_own_sem,
    kv_s,
    kv_r,
    pair_s,
    pair_r,
    far_s,
    far_r,
    cross_s,
    cross_r,
    pass_s,
    pass_r,
    kvg_s,
    kvg_r,
):
    sec = lax.axis_index("sec")
    seq = lax.axis_index("seq")
    mp = lax.axis_index("mp")
    rows, width = q_buf.shape
    cols = x_all.shape[2]
    pieces = pieces_of(cols)
    last = len(pieces) - 1
    own = kv_hbm.shape[1]
    heads = width // DH
    keys = own * seq_n
    kh = heads * keys

    chips = mp_n // 2
    chip, core = mp // 2, mp % 2
    pair = chip * 2 + 1 - core
    far = [
        (((chip + d) % chips) * 2 + core, ((chip + chips - d) % chips) * 2 + core)
        for d in range(1, chips)
    ]
    cross = [(to + 1 - 2 * core, source + 1 - 2 * core) for to, source in far]
    ring = [((seq + d) % seq_n, (seq + seq_n - d) % seq_n) for d in range(1, seq_n)]

    def to_mp(src, dst, send, recv, peer):
        return pltpu.make_async_remote_copy(
            src_ref=src,
            dst_ref=dst,
            send_sem=send,
            recv_sem=recv,
            device_id=(sec, seq, peer),
            device_id_type=MESH,
        )

    def to_seq(src, dst, send, recv, peer):
        return pltpu.make_async_remote_copy(
            src_ref=src,
            dst_ref=dst,
            send_sem=send,
            recv_sem=recv,
            device_id=(sec, peer, mp),
            device_id_type=MESH,
        )

    barrier = pltpu.get_barrier_semaphore()
    for to in [pair] + [to for to, _ in far + cross]:
        pl.semaphore_signal(barrier, inc=1, device_id=(sec, seq, to), device_id_type=MESH)
    for to, _ in ring:
        pl.semaphore_signal(barrier, inc=1, device_id=(sec, to, mp), device_id_type=MESH)

    pl.semaphore_wait(barrier, 1 + 2 * len(far) + len(ring))

    kv_copies = []
    for d, (to, _) in enumerate(ring):
        copy = to_seq(kv_hbm, kv_all.at[seq], kv_s.at[d], kv_r.at[d], to)
        copy.start()
        kv_copies.append(copy)
    far_copies = {}
    for c, (start, end) in enumerate(pieces):
        at = (slice(None), pl.ds(start, end - start))
        for d, (to, _) in enumerate(far):
            copy = to_mp(
                x_hbm.at[at], x_all.at[(mp,) + at], far_s.at[d, c], far_r.at[d, c], to
            )
            copy.start()
            far_copies[d, c] = copy
        if c == 0:
            pair_copy = to_mp(x_hbm, x_all.at[mp], pair_s, pair_r, pair)
            pair_copy.start()
    cross_copies = []
    for d, (to, _) in enumerate(cross):
        copy = to_mp(x_hbm.at[at], x_all.at[(mp,) + at], cross_s.at[d], cross_r.at[d], to)
        copy.start()
        cross_copies.append(copy)

    x_load = pltpu.make_async_copy(x_hbm, x_all.at[mp], x_sem)
    x_load.start()
    kv_load = pltpu.make_async_copy(kv_hbm, kv_all.at[seq], kv_own_sem)
    kv_load.start()
    q_load = pltpu.make_async_copy(q_hbm, q_buf, q_sem)
    q_load.start()
    enc_load = pltpu.make_async_copy(enc_hbm, enc_buf, len_sem.at[0])
    enc_load.start()
    dec_load = pltpu.make_async_copy(dec_hbm, dec_buf, len_sem.at[1])
    dec_load.start()
    order = [mp, pair] + [source for _, source in far + cross]
    w_loads = []
    for n, piece in enumerate(order):
        start = pl.multiple_of(piece * cols, cols)
        load = pltpu.make_async_copy(
            w_hbm.at[:, pl.ds(start, cols)], w_buf.at[piece], w_sem.at[n]
        )
        load.start(priority=1)
        w_loads.append(load)

    kv_load.wait()
    for copy in kv_copies:
        copy.wait_recv()
    for t in range(seq_n):
        for h in range(heads):
            at = pl.ds(h * keys + t * own, own)
            k_rows[at, :] = kv_all[t, 0].astype(jnp.float32)
            v_rows[at, :] = kv_all[t, 1].astype(jnp.float32)
    row_head = lax.broadcasted_iota(jnp.int32, (kh, width), 0) // keys
    col_head = lax.broadcasted_iota(jnp.int32, (kh, width), 1) // DH
    diagonal = row_head == col_head
    k_diag = jnp.where(diagonal, k_rows[...], 0.0).astype(jnp.bfloat16)
    v_diag = jnp.where(diagonal, v_rows[...], 0.0).astype(jnp.bfloat16)

    scale = DH ** (-0.5)
    q_load.wait()
    scores = dot(k_diag, q_buf[...], NT) * scale
    key_at = lax.broadcasted_iota(jnp.int32, (keys, rows), 0)
    token_at = lax.broadcasted_iota(jnp.int32, (1, rows), 1) + seq * rows
    enc_load.wait()
    dec_load.wait()
    allowed = key_at < enc_buf[sec]
    valid = token_at < dec_buf[sec]
    probs = []
    for h in range(heads):
        s = jnp.where(allowed, scores[h * keys : (h + 1) * keys], -1e30)
        e = jnp.where(allowed, jnp.exp(s - jnp.max(s, axis=0, keepdims=True)), 0.0)
        e = e / jnp.sum(e, axis=0, keepdims=True)
        probs.append(jnp.where(valid, e, 0.0))
    prob = jnp.concatenate(probs, axis=0) if heads > 1 else probs[0]
    prob_bf16 = prob.astype(jnp.bfloat16)

    for load, source in zip(w_loads, order):
        load.wait()
        vw_buf[source] = dot(v_diag, w_buf[source], NN).astype(jnp.bfloat16)

    def parts_of(source, piece):
        at = slice(*piece)
        x = x_all[source, :, at]
        grad_prob = dot(vw_buf[source, :, at], x, NT)
        weighted = dot(prob_bf16, x, NN).astype(jnp.bfloat16)
        return grad_prob, dot(weighted, w_buf[source, :, at], NT)

    x_load.wait()
    grad_prob, value_part = parts_of(mp, (0, cols))

    def add(source, piece):
        more_prob, more_value = parts_of(source, piece)
        return grad_prob + more_prob, value_part + more_value

    pair_copy.wait_recv()
    grad_prob, value_part = add(pair, (0, cols))

    pass_copies = {}
    for c, piece in enumerate(pieces):
        for d, (_, source) in enumerate(far):
            far_copies[d, c].wait_recv()
            if c < last:
                slot = x_all.at[source, :, pl.ds(piece[0], piece[1] - piece[0])]
                copy = to_mp(slot, slot, pass_s.at[d, c], pass_r.at[d, c], pair)
                copy.start()
                pass_copies[d, c] = copy
        for _, source in far:
            grad_prob, value_part = add(source, piece)
        if c > 0:
            for d, (_, source) in enumerate(cross):
                pass_copies[d, c - 1].wait_recv()
                grad_prob, value_part = add(source, pieces[c - 1])
    for d, (_, source) in enumerate(cross):
        cross_copies[d].wait_recv()
        grad_prob, value_part = add(source, pieces[last])

    grads = []
    for h in range(heads):
        at = slice(h * keys, (h + 1) * keys)
        delta = jnp.sum(prob[at] * grad_prob[at], axis=0, keepdims=True)
        grads.append(prob[at] * (grad_prob[at] - delta))
    grad_score = (jnp.concatenate(grads, axis=0) if heads > 1 else grads[0]).astype(jnp.bfloat16)
    key_part = dot(grad_score, q_buf[...], NN) * scale

    def own_head(part):
        part = jnp.where(diagonal, part, 0.0)
        return sum(part[h * keys : (h + 1) * keys] for h in range(heads))

    key_part, value_part = own_head(key_part), own_head(value_part)
    for t in range(seq_n):
        kvg_send[t, pl.ds(0, own), :] = key_part[t * own : (t + 1) * own]
        kvg_send[t, pl.ds(own, own), :] = value_part[t * own : (t + 1) * own]
    kvg_copies = []
    for d, (to, _) in enumerate(ring):
        copy = to_seq(kvg_send.at[to], kvg_all.at[seq], kvg_s.at[d], kvg_r.at[d], to)
        copy.start()
        kvg_copies.append(copy)

    qg_ref[...] = (dot(grad_score, k_diag, TN) * scale).astype(jnp.bfloat16)

    sent = kv_copies + [pair_copy] + cross_copies
    for copy in sent + list(far_copies.values()) + list(pass_copies.values()):
        copy.wait_send()

    total = kvg_send[seq]
    for d, (_, source) in enumerate(ring):
        kvg_copies[d].wait_recv()
        total += kvg_all[source]
    kvg_ref[0] = total[:own].astype(jnp.bfloat16)
    kvg_ref[1] = total[own:].astype(jnp.bfloat16)

    for copy in kvg_copies:
        copy.wait_send()


def store_kernel(qg_ref, kvg_ref, qg_hbm, kvg_hbm, sem):
    copies = [
        pltpu.make_async_copy(qg_ref, qg_hbm, sem.at[0]),
        pltpu.make_async_copy(kvg_ref, kvg_hbm, sem.at[1]),
    ]
    for copy in copies:
        copy.start()
    for copy in copies:
        copy.wait()


def body(queries, keys_values, out_grad, out_weight, enc_len, dec_len):
    seq_n, mp_n = lax.axis_size("seq"), lax.axis_size("mp")
    rows, width = queries.shape
    cols = out_grad.shape[1]
    cuts = len(pieces_of(cols))
    own = keys_values.shape[1]
    keys = own * seq_n
    kh = width // DH * keys
    far_n = max(mp_n // 2 - 1, 1)
    bf16, f32 = jnp.bfloat16, jnp.float32
    hbm = pl.BlockSpec(memory_space=pltpu.HBM)
    vmem = pl.BlockSpec(memory_space=pltpu.VMEM)
    dma = pltpu.SemaphoreType.DMA
    operands = [
        pltpu.with_memory_space_constraint(a, pltpu.HBM)
        for a in (enc_len, dec_len, queries, keys_values, out_grad, out_weight)
    ]
    results = pl.pallas_call(
        functools.partial(kernel, seq_n, mp_n),
        out_shape=(
            pltpu.VMEM((rows, width), bf16),
            pltpu.VMEM((2, own, width), bf16),
        ),
        in_specs=[hbm] * 6,
        out_specs=(vmem, vmem),
        scratch_shapes=[
            pltpu.SMEM((SEQS,), jnp.int32),
            pltpu.SMEM((SEQS,), jnp.int32),
            pltpu.VMEM((rows, width), bf16),
            pltpu.VMEM((mp_n, rows, cols), bf16),
            pltpu.VMEM((mp_n, width, cols), bf16),
            pltpu.VMEM((seq_n, 2, own, width), bf16),
            pltpu.VMEM((kh, width), f32),
            pltpu.VMEM((kh, width), f32),
            pltpu.VMEM((mp_n, kh, cols), bf16),
            pltpu.VMEM((seq_n, 2 * own, width), f32),
            pltpu.VMEM((seq_n, 2 * own, width), f32),
            dma((2,)),
            dma,
            dma,
            dma((mp_n,)),
            dma,
            dma((seq_n,)),
            dma((seq_n,)),
            dma,
            dma,
            dma((far_n, cuts)),
            dma((far_n, cuts)),
            dma((far_n,)),
            dma((far_n,)),
            dma((far_n, cuts)),
            dma((far_n, cuts)),
            dma((seq_n,)),
            dma((seq_n,)),
        ],
        compiler_params=pltpu.CompilerParams(
            collective_id=0, has_side_effects=True, vmem_limit_bytes=48 * 2**20
        ),
        name="cross_attention_backward",
    )(*operands)
    results = [pltpu.with_memory_space_constraint(a, pltpu.VMEM) for a in results]
    return pl.pallas_call(
        store_kernel,
        out_shape=(
            jax.ShapeDtypeStruct((rows, width), bf16),
            jax.ShapeDtypeStruct((2, own, width), bf16),
        ),
        in_specs=[vmem, vmem],
        out_specs=(hbm, hbm),
        scratch_shapes=[dma((2,))],
        name="store_results",
    )(*results)


def solution(mesh):
    assert mesh.shape["sec"] == SEQS
    placed = (
        P(("sec", "seq"), "mp"),
        P(None, ("sec", "seq"), "mp"),
        P(("sec", "seq"), "mp"),
        P("mp", None),
        P(),
        P(),
    )
    return jax.shard_map(
        body,
        mesh=mesh,
        in_specs=placed,
        out_specs=(P(("sec", "seq"), "mp"), P(None, ("sec", "seq"), "mp")),
        check_vma=False,
    )
```

```python
import functools

import jax
import jax.numpy as jnp
from jax import lax
from jax.experimental import pallas as pl
from jax.experimental.pallas import tpu as pltpu
from jax.sharding import PartitionSpec as P

DH = 256
SEQS = 2
LANES = 128
MESH = pl.DeviceIdType.MESH
NN = (((1,), (0,)), ((), ()))
NT = (((1,), (1,)), ((), ()))
TN = (((0,), (0,)), ((), ()))


def dot(a, b, dims):
    return lax.dot_general(a, b, dims, preferred_element_type=jnp.float32)


def piece_of(cols):
    return max(cols // 4, LANES)


def kernel(
    seq_n,
    mp_n,
    enc_hbm,
    dec_hbm,
    q_hbm,
    kv_hbm,
    x_hbm,
    w_hbm,
    qg_ref,
    kvg_ref,
    enc_buf,
    dec_buf,
    q_buf,
    x_all,
    w_buf,
    kv_all,
    k_rows,
    v_rows,
    g_sum,
    kvg_send,
    kvg_all,
    len_sem,
    q_sem,
    x_sem,
    w_sem,
    kv_own_sem,
    kv_s,
    kv_r,
    pair_s,
    pair_r,
    far_s,
    far_r,
    pass_s,
    pass_r,
    kvg_s,
    kvg_r,
):
    sec = lax.axis_index("sec")
    seq = lax.axis_index("seq")
    mp = lax.axis_index("mp")
    rows, width = q_buf.shape
    cols = x_all.shape[2]
    piece = piece_of(cols)
    pieces = cols // piece
    own = kv_hbm.shape[1]
    heads = width // DH
    keys = own * seq_n
    kh = heads * keys

    chips = mp_n // 2
    chip, core = mp // 2, mp % 2
    pair = chip * 2 + 1 - core
    far = [
        (((chip + d) % chips) * 2 + core, ((chip + chips - d) % chips) * 2 + core)
        for d in range(1, chips)
    ]
    cross = [(to + 1 - 2 * core, source + 1 - 2 * core) for to, source in far]
    ring = [((seq + d) % seq_n, (seq + seq_n - d) % seq_n) for d in range(1, seq_n)]

    def to_mp(src, dst, send, recv, peer):
        return pltpu.make_async_remote_copy(
            src_ref=src,
            dst_ref=dst,
            send_sem=send,
            recv_sem=recv,
            device_id=(sec, seq, peer),
            device_id_type=MESH,
        )

    def to_seq(src, dst, send, recv, peer):
        return pltpu.make_async_remote_copy(
            src_ref=src,
            dst_ref=dst,
            send_sem=send,
            recv_sem=recv,
            device_id=(sec, peer, mp),
            device_id_type=MESH,
        )

    barrier = pltpu.get_barrier_semaphore()
    for to in [pair] + [to for to, _ in far]:
        pl.semaphore_signal(barrier, inc=1, device_id=(sec, seq, to), device_id_type=MESH)
    for to, _ in ring:
        pl.semaphore_signal(barrier, inc=1, device_id=(sec, to, mp), device_id_type=MESH)

    pl.semaphore_wait(barrier, 1 + len(far) + len(ring))

    kv_copies = []
    for d, (to, _) in enumerate(ring):
        copy = to_seq(kv_hbm, kv_all.at[seq], kv_s.at[d], kv_r.at[d], to)
        copy.start()
        kv_copies.append(copy)
    far_copies = {}
    for c in range(pieces):
        at = (slice(None), pl.ds(c * piece, piece))
        for d, (to, _) in enumerate(far):
            copy = to_mp(
                x_hbm.at[at], x_all.at[(mp,) + at], far_s.at[d, c], far_r.at[d, c], to
            )
            copy.start()
            far_copies[d, c] = copy
        if c == 0:
            pair_copy = to_mp(x_hbm, x_all.at[mp], pair_s, pair_r, pair)
            pair_copy.start()
    kv_load = pltpu.make_async_copy(kv_hbm, kv_all.at[seq], kv_own_sem)
    kv_load.start()
    q_load = pltpu.make_async_copy(q_hbm, q_buf, q_sem)
    q_load.start()
    enc_load = pltpu.make_async_copy(enc_hbm, enc_buf, len_sem.at[0])
    enc_load.start()
    dec_load = pltpu.make_async_copy(dec_hbm, dec_buf, len_sem.at[1])
    dec_load.start()
    x_load = pltpu.make_async_copy(x_hbm, x_all.at[mp], x_sem)
    x_load.start()
    order = [mp, pair] + [source for _, source in far + cross]
    w_loads = []
    for n, source in enumerate(order):
        start = pl.multiple_of(source * cols, cols)
        load = pltpu.make_async_copy(
            w_hbm.at[:, pl.ds(start, cols)], w_buf.at[source], w_sem.at[n]
        )
        load.start()
        w_loads.append(load)

    def columns(c):
        return pl.ds(pl.multiple_of(c * piece, piece), piece)

    def add(source, c):
        at = columns(c)
        g_sum[...] += dot(x_all[source, :, at], w_buf[source, :, at], NT)

    g_sum[...] = jnp.zeros_like(g_sum)
    x_load.wait()
    pair_copy.wait_recv()
    for load in w_loads[:2]:
        load.wait()

    def near_step(n, carry):
        add(jnp.where(n < pieces, mp, pair), lax.rem(n, pieces))
        return carry

    lax.fori_loop(0, 2 * pieces, near_step, 0)

    kv_load.wait()
    for copy in kv_copies:
        copy.wait_recv()
    for t in range(seq_n):
        for h in range(heads):
            at = pl.ds(h * keys + t * own, own)
            k_rows[at, :] = kv_all[t, 0].astype(jnp.float32)
            v_rows[at, :] = kv_all[t, 1].astype(jnp.float32)
    row_head = lax.broadcasted_iota(jnp.int32, (kh, width), 0) // keys
    col_head = lax.broadcasted_iota(jnp.int32, (kh, width), 1) // DH
    diagonal = row_head == col_head
    k_diag = jnp.where(diagonal, k_rows[...], 0.0).astype(jnp.bfloat16)
    v_diag = jnp.where(diagonal, v_rows[...], 0.0).astype(jnp.bfloat16)

    scale = DH ** (-0.5)
    q_load.wait()
    scores = dot(k_diag, q_buf[...], NT) * scale
    key_at = lax.broadcasted_iota(jnp.int32, (keys, rows), 0)
    token_at = lax.broadcasted_iota(jnp.int32, (1, rows), 1) + seq * rows
    enc_load.wait()
    dec_load.wait()
    allowed = key_at < enc_buf[sec]
    valid = token_at < dec_buf[sec]
    probs = []
    for h in range(heads):
        s = jnp.where(allowed, scores[h * keys : (h + 1) * keys], -1e30)
        e = jnp.where(allowed, jnp.exp(s - jnp.max(s, axis=0, keepdims=True)), 0.0)
        e = e / jnp.sum(e, axis=0, keepdims=True)
        probs.append(jnp.where(valid, e, 0.0))
    prob = jnp.concatenate(probs, axis=0) if heads > 1 else probs[0]
    prob_bf16 = prob.astype(jnp.bfloat16)

    for load in w_loads[2:]:
        load.wait()

    def handing_on(d, c):
        slot = x_all.at[far[d][1], :, columns(c)]
        return to_mp(slot, slot, pass_s.at[d, c], pass_r.at[d, c], pair)

    def arriving(d, c):
        slot = x_all.at[far[d][1], :, columns(c)]
        return to_mp(slot, slot, far_s.at[d, c], far_r.at[d, c], far[d][0])

    def far_step(c, carry):
        for d in range(len(far)):
            arriving(d, c).wait_recv()
            handing_on(d, c).start()
        for _, source in far:
            add(source, c)
        for d, (_, source) in enumerate(cross):
            handing_on(d, c).wait_recv()
            add(source, c)
        return carry

    lax.fori_loop(0, pieces, far_step, 0)
    g = g_sum[...].astype(jnp.bfloat16)

    value_part = dot(prob_bf16, g, NN)
    grad_prob = dot(v_diag, g, NT)
    grads = []
    for h in range(heads):
        at = slice(h * keys, (h + 1) * keys)
        delta = jnp.sum(prob[at] * grad_prob[at], axis=0, keepdims=True)
        grads.append(prob[at] * (grad_prob[at] - delta))
    grad_score = (jnp.concatenate(grads, axis=0) if heads > 1 else grads[0]).astype(jnp.bfloat16)
    key_part = dot(grad_score, q_buf[...], NN) * scale

    def own_head(part):
        part = jnp.where(diagonal, part, 0.0)
        return sum(part[h * keys : (h + 1) * keys] for h in range(heads))

    key_part, value_part = own_head(key_part), own_head(value_part)
    for t in range(seq_n):
        kvg_send[t, pl.ds(0, own), :] = key_part[t * own : (t + 1) * own]
        kvg_send[t, pl.ds(own, own), :] = value_part[t * own : (t + 1) * own]
    kvg_copies = []
    for d, (to, _) in enumerate(ring):
        copy = to_seq(kvg_send.at[to], kvg_all.at[seq], kvg_s.at[d], kvg_r.at[d], to)
        copy.start()
        kvg_copies.append(copy)

    qg_ref[...] = (dot(grad_score, k_diag, TN) * scale).astype(jnp.bfloat16)

    for copy in kv_copies + [pair_copy] + list(far_copies.values()):
        copy.wait_send()
    for d in range(len(far)):
        for c in range(pieces):
            handing_on(d, c).wait_send()

    total = kvg_send[seq]
    for d, (_, source) in enumerate(ring):
        kvg_copies[d].wait_recv()
        total += kvg_all[source]
    kvg_ref[0] = total[:own].astype(jnp.bfloat16)
    kvg_ref[1] = total[own:].astype(jnp.bfloat16)

    for copy in kvg_copies:
        copy.wait_send()


def store_kernel(qg_ref, kvg_ref, qg_hbm, kvg_hbm, sem):
    copies = [
        pltpu.make_async_copy(qg_ref, qg_hbm, sem.at[0]),
        pltpu.make_async_copy(kvg_ref, kvg_hbm, sem.at[1]),
    ]
    for copy in copies:
        copy.start()
    for copy in copies:
        copy.wait()


def body(queries, keys_values, out_grad, out_weight, enc_len, dec_len):
    seq_n, mp_n = lax.axis_size("seq"), lax.axis_size("mp")
    rows, width = queries.shape
    cols = out_grad.shape[1]
    cuts = cols // piece_of(cols)
    own = keys_values.shape[1]
    keys = own * seq_n
    kh = width // DH * keys
    far_n = max(mp_n // 2 - 1, 1)
    bf16, f32 = jnp.bfloat16, jnp.float32
    hbm = pl.BlockSpec(memory_space=pltpu.HBM)
    vmem = pl.BlockSpec(memory_space=pltpu.VMEM)
    dma = pltpu.SemaphoreType.DMA
    operands = [
        pltpu.with_memory_space_constraint(a, pltpu.HBM)
        for a in (enc_len, dec_len, queries, keys_values, out_grad, out_weight)
    ]
    results = pl.pallas_call(
        functools.partial(kernel, seq_n, mp_n),
        out_shape=(
            pltpu.VMEM((rows, width), bf16),
            pltpu.VMEM((2, own, width), bf16),
        ),
        in_specs=[hbm] * 6,
        out_specs=(vmem, vmem),
        scratch_shapes=[
            pltpu.SMEM((SEQS,), jnp.int32),
            pltpu.SMEM((SEQS,), jnp.int32),
            pltpu.VMEM((rows, width), bf16),
            pltpu.VMEM((mp_n, rows, cols), bf16),
            pltpu.VMEM((mp_n, width, cols), bf16),
            pltpu.VMEM((seq_n, 2, own, width), bf16),
            pltpu.VMEM((kh, width), f32),
            pltpu.VMEM((kh, width), f32),
            pltpu.VMEM((rows, width), f32),
            pltpu.VMEM((seq_n, 2 * own, width), f32),
            pltpu.VMEM((seq_n, 2 * own, width), f32),
            dma((2,)),
            dma,
            dma,
            dma((mp_n,)),
            dma,
            dma((seq_n,)),
            dma((seq_n,)),
            dma,
            dma,
            dma((far_n, cuts)),
            dma((far_n, cuts)),
            dma((far_n, cuts)),
            dma((far_n, cuts)),
            dma((seq_n,)),
            dma((seq_n,)),
        ],
        compiler_params=pltpu.CompilerParams(
            collective_id=0, has_side_effects=True, vmem_limit_bytes=48 * 2**20
        ),
        name="cross_attention_backward",
    )(*operands)
    results = [pltpu.with_memory_space_constraint(a, pltpu.VMEM) for a in results]
    return pl.pallas_call(
        store_kernel,
        out_shape=(
            jax.ShapeDtypeStruct((rows, width), bf16),
            jax.ShapeDtypeStruct((2, own, width), bf16),
        ),
        in_specs=[vmem, vmem],
        out_specs=(hbm, hbm),
        scratch_shapes=[dma((2,))],
        name="store_results",
    )(*results)


def solution(mesh):
    assert mesh.shape["sec"] == SEQS
    placed = (
        P(("sec", "seq"), "mp"),
        P(None, ("sec", "seq"), "mp"),
        P(("sec", "seq"), "mp"),
        P("mp", None),
        P(),
        P(),
    )
    return jax.shard_map(
        body,
        mesh=mesh,
        in_specs=placed,
        out_specs=(P(("sec", "seq"), "mp"), P(None, ("sec", "seq"), "mp")),
        check_vma=False,
    )
```

```python
import functools

import jax
import jax.numpy as jnp
from jax import lax
from jax.experimental import pallas as pl
from jax.experimental.pallas import tpu as pltpu
from jax.sharding import PartitionSpec as P

DH = 256
SEQS = 2
LANES = 128
MESH = pl.DeviceIdType.MESH
NN = (((1,), (0,)), ((), ()))
NT = (((1,), (1,)), ((), ()))
TN = (((0,), (0,)), ((), ()))


def dot(a, b, dims):
    return lax.dot_general(a, b, dims, preferred_element_type=jnp.float32)


def pieces_of(cols):
    edges = list(range(0, cols, max(cols // 4, LANES))) + [cols]
    middle = (edges[-2] + cols) // 2
    if middle % LANES == 0 and middle > edges[-2]:
        edges.insert(-1, middle)
    return list(zip(edges[:-1], edges[1:]))


def kernel(
    seq_n,
    mp_n,
    enc_hbm,
    dec_hbm,
    q_hbm,
    kv_hbm,
    x_hbm,
    w_hbm,
    qg_ref,
    kvg_ref,
    enc_buf,
    dec_buf,
    q_buf,
    x_all,
    w_buf,
    kv_all,
    k_rows,
    v_rows,
    g_sum,
    kvg_send,
    kvg_all,
    len_sem,
    q_sem,
    x_sem,
    w_sem,
    kv_own_sem,
    kv_s,
    kv_r,
    pair_s,
    pair_r,
    far_s,
    far_r,
    cross_s,
    cross_r,
    pass_s,
    pass_r,
    kvg_s,
    kvg_r,
):
    sec = lax.axis_index("sec")
    seq = lax.axis_index("seq")
    mp = lax.axis_index("mp")
    rows, width = q_buf.shape
    cols = x_all.shape[2]
    pieces = pieces_of(cols)
    last = len(pieces) - 1
    own = kv_hbm.shape[1]
    heads = width // DH
    keys = own * seq_n
    kh = heads * keys

    chips = mp_n // 2
    chip, core = mp // 2, mp % 2
    pair = chip * 2 + 1 - core
    far = [
        (((chip + d) % chips) * 2 + core, ((chip + chips - d) % chips) * 2 + core)
        for d in range(1, chips)
    ]
    cross = [(to + 1 - 2 * core, source + 1 - 2 * core) for to, source in far]
    ring = [((seq + d) % seq_n, (seq + seq_n - d) % seq_n) for d in range(1, seq_n)]

    def to_mp(src, dst, send, recv, peer):
        return pltpu.make_async_remote_copy(
            src_ref=src,
            dst_ref=dst,
            send_sem=send,
            recv_sem=recv,
            device_id=(sec, seq, peer),
            device_id_type=MESH,
        )

    def to_seq(src, dst, send, recv, peer):
        return pltpu.make_async_remote_copy(
            src_ref=src,
            dst_ref=dst,
            send_sem=send,
            recv_sem=recv,
            device_id=(sec, peer, mp),
            device_id_type=MESH,
        )

    barrier = pltpu.get_barrier_semaphore()
    for to in [pair] + [to for to, _ in far + cross]:
        pl.semaphore_signal(barrier, inc=1, device_id=(sec, seq, to), device_id_type=MESH)
    for to, _ in ring:
        pl.semaphore_signal(barrier, inc=1, device_id=(sec, to, mp), device_id_type=MESH)

    pl.semaphore_wait(barrier, 1 + 2 * len(far) + len(ring))

    kv_copies = []
    for d, (to, _) in enumerate(ring):
        copy = to_seq(kv_hbm, kv_all.at[seq], kv_s.at[d], kv_r.at[d], to)
        copy.start()
        kv_copies.append(copy)
    far_copies = {}
    for c, (start, end) in enumerate(pieces):
        at = (slice(None), pl.ds(start, end - start))
        for d, (to, _) in enumerate(far):
            copy = to_mp(
                x_hbm.at[at], x_all.at[(mp,) + at], far_s.at[d, c], far_r.at[d, c], to
            )
            copy.start()
            far_copies[d, c] = copy
        if c == 0:
            pair_copy = to_mp(x_hbm, x_all.at[mp], pair_s, pair_r, pair)
            pair_copy.start()
    cross_copies = []
    for d, (to, _) in enumerate(cross):
        copy = to_mp(x_hbm.at[at], x_all.at[(mp,) + at], cross_s.at[d], cross_r.at[d], to)
        copy.start()
        cross_copies.append(copy)

    kv_load = pltpu.make_async_copy(kv_hbm, kv_all.at[seq], kv_own_sem)
    kv_load.start()
    q_load = pltpu.make_async_copy(q_hbm, q_buf, q_sem)
    q_load.start()
    enc_load = pltpu.make_async_copy(enc_hbm, enc_buf, len_sem.at[0])
    enc_load.start()
    dec_load = pltpu.make_async_copy(dec_hbm, dec_buf, len_sem.at[1])
    dec_load.start()
    x_load = pltpu.make_async_copy(x_hbm, x_all.at[mp], x_sem)
    x_load.start()
    order = [mp, pair] + [source for _, source in far + cross]
    w_loads = []
    for n, piece in enumerate(order):
        start = pl.multiple_of(piece * cols, cols)
        load = pltpu.make_async_copy(
            w_hbm.at[:, pl.ds(start, cols)], w_buf.at[piece], w_sem.at[n]
        )
        load.start(priority=1)
        w_loads.append(load)

    def part_of(source, piece):
        at = slice(*piece)
        return dot(x_all[source, :, at], w_buf[source, :, at], NT)

    x_load.wait()
    w_loads[0].wait()
    g_sum[...] = part_of(mp, (0, cols))
    pair_copy.wait_recv()
    w_loads[1].wait()
    g_sum[...] += part_of(pair, (0, cols))

    kv_load.wait()
    for copy in kv_copies:
        copy.wait_recv()
    for t in range(seq_n):
        for h in range(heads):
            at = pl.ds(h * keys + t * own, own)
            k_rows[at, :] = kv_all[t, 0].astype(jnp.float32)
            v_rows[at, :] = kv_all[t, 1].astype(jnp.float32)
    row_head = lax.broadcasted_iota(jnp.int32, (kh, width), 0) // keys
    col_head = lax.broadcasted_iota(jnp.int32, (kh, width), 1) // DH
    diagonal = row_head == col_head
    k_diag = jnp.where(diagonal, k_rows[...], 0.0).astype(jnp.bfloat16)
    v_diag = jnp.where(diagonal, v_rows[...], 0.0).astype(jnp.bfloat16)

    scale = DH ** (-0.5)
    q_load.wait()
    scores = dot(k_diag, q_buf[...], NT) * scale
    key_at = lax.broadcasted_iota(jnp.int32, (keys, rows), 0)
    token_at = lax.broadcasted_iota(jnp.int32, (1, rows), 1) + seq * rows
    enc_load.wait()
    dec_load.wait()
    allowed = key_at < enc_buf[sec]
    valid = token_at < dec_buf[sec]
    probs = []
    for h in range(heads):
        s = jnp.where(allowed, scores[h * keys : (h + 1) * keys], -1e30)
        e = jnp.where(allowed, jnp.exp(s - jnp.max(s, axis=0, keepdims=True)), 0.0)
        e = e / jnp.sum(e, axis=0, keepdims=True)
        probs.append(jnp.where(valid, e, 0.0))
    prob = jnp.concatenate(probs, axis=0) if heads > 1 else probs[0]
    prob_bf16 = prob.astype(jnp.bfloat16)

    for load in w_loads[2:]:
        load.wait()
    pass_copies = {}
    for c, piece in enumerate(pieces):
        for d, (_, source) in enumerate(far):
            far_copies[d, c].wait_recv()
            if c < last:
                slot = x_all.at[source, :, pl.ds(piece[0], piece[1] - piece[0])]
                copy = to_mp(slot, slot, pass_s.at[d, c], pass_r.at[d, c], pair)
                copy.start()
                pass_copies[d, c] = copy
        total = g_sum[...]
        for _, source in far:
            total += part_of(source, piece)
        if c > 0:
            for d, (_, source) in enumerate(cross):
                pass_copies[d, c - 1].wait_recv()
                total += part_of(source, pieces[c - 1])
        if c < last:
            g_sum[...] = total
    for d, (_, source) in enumerate(cross):
        cross_copies[d].wait_recv()
        total += part_of(source, pieces[last])
    g = total.astype(jnp.bfloat16)

    value_part = dot(prob_bf16, g, NN)
    grad_prob = dot(v_diag, g, NT)
    grads = []
    for h in range(heads):
        at = slice(h * keys, (h + 1) * keys)
        delta = jnp.sum(prob[at] * grad_prob[at], axis=0, keepdims=True)
        grads.append(prob[at] * (grad_prob[at] - delta))
    grad_score = (jnp.concatenate(grads, axis=0) if heads > 1 else grads[0]).astype(jnp.bfloat16)
    key_part = dot(grad_score, q_buf[...], NN) * scale

    def own_head(part):
        part = jnp.where(diagonal, part, 0.0)
        return sum(part[h * keys : (h + 1) * keys] for h in range(heads))

    key_part, value_part = own_head(key_part), own_head(value_part)
    for t in range(seq_n):
        kvg_send[t, pl.ds(0, own), :] = key_part[t * own : (t + 1) * own]
        kvg_send[t, pl.ds(own, own), :] = value_part[t * own : (t + 1) * own]
    kvg_copies = []
    for d, (to, _) in enumerate(ring):
        copy = to_seq(kvg_send.at[to], kvg_all.at[seq], kvg_s.at[d], kvg_r.at[d], to)
        copy.start()
        kvg_copies.append(copy)

    qg_ref[...] = (dot(grad_score, k_diag, TN) * scale).astype(jnp.bfloat16)

    sent = kv_copies + [pair_copy] + cross_copies
    for copy in sent + list(far_copies.values()) + list(pass_copies.values()):
        copy.wait_send()

    total = kvg_send[seq]
    for d, (_, source) in enumerate(ring):
        kvg_copies[d].wait_recv()
        total += kvg_all[source]
    kvg_ref[0] = total[:own].astype(jnp.bfloat16)
    kvg_ref[1] = total[own:].astype(jnp.bfloat16)

    for copy in kvg_copies:
        copy.wait_send()


def store_kernel(qg_ref, kvg_ref, qg_hbm, kvg_hbm, sem):
    copies = [
        pltpu.make_async_copy(qg_ref, qg_hbm, sem.at[0]),
        pltpu.make_async_copy(kvg_ref, kvg_hbm, sem.at[1]),
    ]
    for copy in copies:
        copy.start()
    for copy in copies:
        copy.wait()


def body(queries, keys_values, out_grad, out_weight, enc_len, dec_len):
    seq_n, mp_n = lax.axis_size("seq"), lax.axis_size("mp")
    rows, width = queries.shape
    cols = out_grad.shape[1]
    cuts = len(pieces_of(cols))
    own = keys_values.shape[1]
    keys = own * seq_n
    kh = width // DH * keys
    far_n = max(mp_n // 2 - 1, 1)
    bf16, f32 = jnp.bfloat16, jnp.float32
    hbm = pl.BlockSpec(memory_space=pltpu.HBM)
    vmem = pl.BlockSpec(memory_space=pltpu.VMEM)
    dma = pltpu.SemaphoreType.DMA
    operands = [
        pltpu.with_memory_space_constraint(a, pltpu.HBM)
        for a in (enc_len, dec_len, queries, keys_values, out_grad, out_weight)
    ]
    results = pl.pallas_call(
        functools.partial(kernel, seq_n, mp_n),
        out_shape=(
            pltpu.VMEM((rows, width), bf16),
            pltpu.VMEM((2, own, width), bf16),
        ),
        in_specs=[hbm] * 6,
        out_specs=(vmem, vmem),
        scratch_shapes=[
            pltpu.SMEM((SEQS,), jnp.int32),
            pltpu.SMEM((SEQS,), jnp.int32),
            pltpu.VMEM((rows, width), bf16),
            pltpu.VMEM((mp_n, rows, cols), bf16),
            pltpu.VMEM((mp_n, width, cols), bf16),
            pltpu.VMEM((seq_n, 2, own, width), bf16),
            pltpu.VMEM((kh, width), f32),
            pltpu.VMEM((kh, width), f32),
            pltpu.VMEM((rows, width), f32),
            pltpu.VMEM((seq_n, 2 * own, width), f32),
            pltpu.VMEM((seq_n, 2 * own, width), f32),
            dma((2,)),
            dma,
            dma,
            dma((mp_n,)),
            dma,
            dma((seq_n,)),
            dma((seq_n,)),
            dma,
            dma,
            dma((far_n, cuts)),
            dma((far_n, cuts)),
            dma((far_n,)),
            dma((far_n,)),
            dma((far_n, cuts)),
            dma((far_n, cuts)),
            dma((seq_n,)),
            dma((seq_n,)),
        ],
        compiler_params=pltpu.CompilerParams(
            collective_id=0, has_side_effects=True, vmem_limit_bytes=48 * 2**20
        ),
        name="cross_attention_backward",
    )(*operands)
    results = [pltpu.with_memory_space_constraint(a, pltpu.VMEM) for a in results]
    return pl.pallas_call(
        store_kernel,
        out_shape=(
            jax.ShapeDtypeStruct((rows, width), bf16),
            jax.ShapeDtypeStruct((2, own, width), bf16),
        ),
        in_specs=[vmem, vmem],
        out_specs=(hbm, hbm),
        scratch_shapes=[dma((2,))],
        name="store_results",
    )(*results)


def solution(mesh):
    assert mesh.shape["sec"] == SEQS
    placed = (
        P(("sec", "seq"), "mp"),
        P(None, ("sec", "seq"), "mp"),
        P(("sec", "seq"), "mp"),
        P("mp", None),
        P(),
        P(),
    )
    return jax.shard_map(
        body,
        mesh=mesh,
        in_specs=placed,
        out_specs=(P(("sec", "seq"), "mp"), P(None, ("sec", "seq"), "mp")),
        check_vma=False,
    )
```
